256 devices in a mesh: item: 32 (over x, z), cent: 8 (over y, core).
Axes of the slice: x: 4, y: 4, z: 8, core: 2. Of those that a mesh axis runs over, the one named last changes fastest.
Arguments:
- vectors: float32 [32768, 256], P('item'), may hold values from -15 to 15, as said below
- centroids: float32 [32768, 256], P('cent'), may hold values from -15 to 15, as said below
Outputs:
- refined: float32 [32768, 256], P('cent')
- log_partition: float32 [32768], P('item')
The draws below stay inside these ranges and needn't reach their ends.
Inputs may be any that keep to these rules, and one draw needn't show every extreme that they name: Entries of order one; a few vectors lie on or near centroids, with large norms. Entries of order one or less; a few centroids are larger.
All inputs are finite; a program needn't handle non-finite values.
Results may differ from the reference program's by a relative error of at most 0.0001.
Values sent between devices are 32-bit elements; how exact they have to be, the bound alone decides.
A program may use at most 128 MiB of HBM per device.

```python
import jax
import jax.numpy as jnp
from jax import lax

EMBED_WIDTH = 256
K = 32768
TOK_DEV = 1024
ITEMS = 32768


def drawn_rows():
    count = ITEMS // TOK_DEV
    index = jnp.arange(count, dtype=jnp.int32)
    target = index * 74 % K
    strength = 150.0 + 100.0 * (index % 3).astype(jnp.float32)
    dispersion_level = jnp.sqrt(24.0 * strength / EMBED_WIDTH)
    return (index, target, strength, dispersion_level)


def shared_base(key):
    return jax.random.uniform(jax.random.fold_in(key, 5), (K, EMBED_WIDTH), jnp.float32, -1.0, 1.0)


def draw_centroids(key, part):
    base = shared_base(key)
    key = jax.random.fold_in(key, 11)
    values = 0.5 * jax.random.normal(key, (K, EMBED_WIDTH), jnp.float32)
    index, target, strength, dispersion_level = drawn_rows()
    displacement_length = jnp.sqrt(2.0 / strength)
    rows = base[target] * dispersion_level[:, None]
    values = values.at[target].set(rows)
    values = values.at[target + 1].set(rows * (1.0 + displacement_length)[:, None])
    return jnp.clip(values, -15.0, 15.0)


def draw_vectors(key, part):
    base = shared_base(key)
    key = jax.random.fold_in(key, 12)
    values = jax.random.normal(key, (ITEMS, EMBED_WIDTH), jnp.float32)
    index, target, strength, dispersion_level = drawn_rows()
    places = index * TOK_DEV + 7 % TOK_DEV
    values = values.at[places].set(base[target] * dispersion_level[:, None])
    return jnp.clip(values, -15.0, 15.0)


def setup_inputs(seed: int = 0) -> dict:
    keys = jax.random.split(jax.random.key(seed), 3)
    return {
        "vectors": draw_vectors(jax.random.fold_in(keys[2], 71), 0),
        "centroids": draw_centroids(jax.random.fold_in(keys[2], 71), 0),
    }


BOLTZMANN_SCALE = 8.0
PRIOR = 2.0


def reference(vectors, centroids):
    center_energy = jnp.sum(centroids * centroids, axis=1)
    blocks = vectors.reshape(ITEMS // TOK_DEV, TOK_DEV, EMBED_WIDTH)

    def one_block(carry, block):
        numer, weight = carry
        inner_pairings = jnp.dot(block, centroids.T, precision=lax.Precision.HIGHEST, preferred_element_type=jnp.float32)
        cluster_affinity_scores = (2.0 * inner_pairings - center_energy[None, :]) / BOLTZMANN_SCALE
        row_max = jnp.max(cluster_affinity_scores, axis=1)
        row_sum = jnp.sum(jnp.exp(cluster_affinity_scores - row_max[:, None]), axis=1)
        lse = row_max + jnp.log(row_sum)
        probs = jnp.exp(cluster_affinity_scores - lse[:, None])
        numer = numer + lax.dot_general(probs, block, (((0,), (0,)), ((), ())), precision=lax.Precision.HIGHEST, preferred_element_type=jnp.float32)
        weight = weight + jnp.sum(probs, axis=0)
        return (numer, weight), lse

    start = (jnp.zeros((K, EMBED_WIDTH), jnp.float32), jnp.zeros((K,), jnp.float32))
    (numer, weight), lses = lax.scan(one_block, start, blocks)
    refined = (numer + PRIOR * centroids) / (weight[:, None] + PRIOR)
    return refined, lses.reshape(ITEMS)
```

```python
import functools
import math

import jax
import jax.numpy as jnp
from jax import lax
from jax.experimental import pallas as pl
from jax.experimental.pallas import tpu as pltpu
from jax.sharding import PartitionSpec as P

MESH = pl.DeviceIdType.MESH
BOLTZMANN_SCALE = 8.0
PRIOR = 2.0
LOG2E = math.log2(math.e)
LN2 = math.log(2.0)
XSCALE = 2.0 * LOG2E / BOLTZMANN_SCALE

NX, NZ, NC = 4, 8, 8
D = 256
N = 1024
KP = 4096
RA, RB = 80, 48
CA, CB = NZ * RA, NX * RB
B0 = NX * CA
TILE = 512
NT = KP // TILE
G = 64

STAT = 0
W1 = STAT + 7
W2 = W1 + 3
A1 = W2 + 7
A2 = A1 + 16
AZ = A2 + 16
BZ = AZ + 8
BX = BZ + 8
GAZ = BX + 4
GA1 = GAZ + 8
GA2 = GA1 + 16
GBX = GA2 + 16
GBZ = GBX + 4
NSEM = GBZ + 8

ORDER_RS = (4, 3, -3, 2, -2, 1, -1, 0)
ORDER_AG = (0, -1, 1, -2, 2, -3, 3, 4)


def dot(a, b):
    return jnp.dot(a, b, preferred_element_type=jnp.float32)


def split(v):
    hi = v.astype(jnp.bfloat16)
    lo = (v - hi.astype(jnp.float32)).astype(jnp.bfloat16)
    return hi, lo


def kernel(
    x_hbm, c_hbm, out, lse_out,
    xbuf, cbuf, xh, xl, xht, xlt, e_buf, m_buf, s_buf, f_buf, stat, numer, w8,
    wown, rw1, w2s, rw2, ra1, ra2, raz0, raz, rbz0, rbz, rbx0, rbx, den,
    ss, rs, lsem,
):
    item = lax.axis_index("item")
    cent = lax.axis_index("cent")
    x, z = item // NZ, lax.rem(item, NZ)

    def mod(v, n):
        return lax.rem(v + 2 * n, n)

    def at_x(d):
        return {"item": mod(x + d, NX) * NZ + z}

    def at_z(d):
        return {"item": x * NZ + mod(z + d, NZ)}

    def at_c(d):
        return {"cent": mod(cent + d, NC)}

    pending = []

    def copy(src, dst, k, dev):
        return pltpu.make_async_remote_copy(
            src_ref=src, dst_ref=dst, send_sem=ss.at[k], recv_sem=rs.at[k],
            device_id=dev, device_id_type=MESH,
        )

    def send(src, dst, k, dev):
        c = copy(src, dst, k, dev)
        c.start()
        pending.append(c)

    def got(region, k):
        copy(region, region, k, at_x(1)).wait_recv()

    x_load = pltpu.make_async_copy(x_hbm, xbuf, lsem.at[NT])
    x_load.start()

    def c_load(t):
        rows = pl.ds(t * TILE, TILE)
        return pltpu.make_async_copy(c_hbm.at[rows], cbuf.at[rows], lsem.at[t])

    for t in range(NT):
        c_load(t).start()

    barrier = pltpu.get_barrier_semaphore()
    for d in range(1, NX):
        pl.semaphore_signal(barrier, inc=1, device_id=at_x(d), device_id_type=MESH)
    for d in range(1, NZ):
        pl.semaphore_signal(barrier, inc=1, device_id=at_z(d), device_id_type=MESH)
    for d in range(1, NC):
        pl.semaphore_signal(barrier, inc=1, device_id=at_c(d), device_id_type=MESH)

    x_load.wait()
    for j in range(N // 256):
        rows = pl.ds(j * 256, 256)
        v = xbuf[rows, :] * XSCALE
        hi, lo = split(v)
        xh[rows, :] = hi
        xl[rows, :] = lo
        hi, lo = split(v.T)
        xht[:, rows] = hi
        xlt[:, rows] = lo

    def tile_a(t, _):
        c_load(t).wait()
        rows = pl.ds(pl.multiple_of(t * TILE, TILE), TILE)
        c = cbuf[rows, :]
        csq = jnp.sum(c * c, axis=1, keepdims=True) * (LOG2E / BOLTZMANN_SCALE)
        ch, cl = split(c)
        for j in range(N // 256):
            cols = pl.ds(j * 256, 256)
            b = xht[:, cols]
            l = dot(ch, b) + dot(cl, b) + dot(ch, xlt[:, cols]) - csq
            l = l.reshape(TILE // 8, 8, 256)
            m = jnp.max(l, axis=0)
            e = jnp.exp2(l - m[None])
            s = jnp.sum(e, axis=0)
            e_buf[rows, cols] = e.reshape(TILE, 256)
            m_buf[t, :, cols] = m
            s_buf[t, :, cols] = s
        return 0

    lax.fori_loop(0, NT, tile_a, 0)

    mm = m_buf[...]
    m_loc = jnp.max(jnp.max(mm, axis=0), axis=0, keepdims=True)
    s_loc = jnp.sum(
        jnp.sum(s_buf[...] * jnp.exp2(mm - m_loc[None]), axis=0), axis=0, keepdims=True
    )
    stat[cent] = m_loc + jnp.log(s_loc) * LOG2E
    pl.semaphore_wait(barrier, (NX - 1) + (NZ - 1) + (NC - 1))
    for d in range(1, NC):
        send(stat.at[cent], stat.at[cent], STAT + d - 1, at_c(d))
    for d in range(1, NC):
        got(stat.at[mod(cent - d, NC)], STAT + d - 1)
    parts = stat[...]
    top = jnp.max(parts, axis=0)
    total = jnp.log(jnp.sum(jnp.exp2(parts - top[None]), axis=0))
    lse_out[...] = top * LN2 + total
    lse2 = top + total * LOG2E
    f_buf[...] = jnp.exp2(mm - lse2[None])

    def block_b(r0, rows_n):
        rows = pl.ds(pl.multiple_of(r0, G), rows_n)
        hs, ls, ws = [], [], []
        for g in range(rows_n // G):
            start = pl.multiple_of(r0 + g * G, G)
            p = e_buf[pl.ds(start, G), :].reshape(G // 8, 8, N) * f_buf[start // TILE][None]
            p = p.reshape(G, N)
            w = p[:, 0:128]
            for q in range(1, N // 128):
                w = w + p[:, q * 128 : (q + 1) * 128]
            w8[pl.ds(start, G), :] = w
            hi, lo = split(p)
            hs.append(hi)
            ls.append(lo)
        hi = jnp.concatenate(hs, axis=0)
        lo = jnp.concatenate(ls, axis=0)
        numer[rows, :] = dot(hi, xh[...]) + dot(lo, xh[...]) + dot(hi, xl[...])

    def chunk_a(d):
        base = mod(x + d, NX) * CA

        def body(i, _):
            block_b(base + i * (CA // 2), CA // 2)
            return 0

        lax.fori_loop(0, 2, body, 0)

    def chunks_b(d0, n):
        def body(i, _):
            block_b(B0 + mod(z + d0 + i, NZ) * CB, CB)
            return 0

        lax.fori_loop(0, n, body, 0)

    def rows_a(dx, dz, off=0, n=RA):
        return pl.ds(pl.multiple_of(mod(x + dx, NX) * CA + mod(z + dz, NZ) * RA + off, 8), n)

    def rows_b(dz, dx, off=0, n=RB):
        return pl.ds(pl.multiple_of(B0 + mod(z + dz, NZ) * CB + mod(x + dx, NX) * RB + off, 8), n)

    def chunk_rows_b(dz, off=0, n=CB):
        return pl.ds(pl.multiple_of(B0 + mod(z + dz, NZ) * CB + off, 8), n)

    def add(rows, ref):
        numer[rows, :] += ref[...]

    HA, HB, HC = RA // 2, RB // 2, CB // 2

    chunk_a(2)
    for i, o in enumerate(ORDER_RS):
        send(numer.at[rows_a(2, o, 0, HA)], ra1.at[0, i], A1 + i, at_x(1))
        send(numer.at[rows_a(2, o, HA, HA)], ra1.at[1, i], A1 + 8 + i, at_x(-1))
    chunks_b(4, 1)
    send(numer.at[chunk_rows_b(4, 0, HC)], rbz0.at[0], BZ, at_z(1))
    send(numer.at[chunk_rows_b(4, HC, HC)], rbz0.at[1], BZ + 4, at_z(-1))
    chunks_b(3, 1)
    chunks_b(-3, 1)
    chunk_a(1)

    def bz_step(k):
        if k == 1:
            got(rbz0.at[0], BZ)
            add(chunk_rows_b(3, 0, HC), rbz0.at[0])
        else:
            got(rbz.at[k - 2, 0], BZ + k - 1)
            add(chunk_rows_b(4 - k), rbz.at[k - 2, 0])
        send(numer.at[chunk_rows_b(4 - k)], rbz.at[k - 1, 0], BZ + k, at_z(1))
        if k == 1:
            got(rbz0.at[1], BZ + 4)
            add(chunk_rows_b(-3, HC, HC), rbz0.at[1])
        else:
            got(rbz.at[k - 2, 1], BZ + 4 + k - 1)
            add(chunk_rows_b(k - 4), rbz.at[k - 2, 1])
        send(numer.at[chunk_rows_b(k - 4)], rbz.at[k - 1, 1], BZ + 4 + k, at_z(-1))

    bz_step(1)
    chunk_a(-1)
    chunks_b(-2, 5)
    chunk_a(0)

    def owner_weights(i, _):
        xd, zd = i // NZ, lax.rem(i, NZ)
        a = w8[pl.ds(pl.multiple_of(xd * CA + zd * RA, 8), RA), :]
        b = w8[pl.ds(pl.multiple_of(B0 + zd * CB + xd * RB, 8), RB), :]
        t = jnp.concatenate([a, b], axis=0).T
        wown[xd, pl.ds(zd, 1), :] = jnp.sum(t, axis=0, keepdims=True)
        return 0

    lax.fori_loop(0, NX * NZ, owner_weights, 0)
    for d in range(1, NX):
        send(wown.at[mod(x + d, NX)], rw1.at[d - 1], W1 + d - 1, at_x(d))

    def a1_step(i):
        o = ORDER_RS[i]
        got(ra1.at[0, i], A1 + i)
        add(rows_a(1, o, 0, HA), ra1.at[0, i])
        send(numer.at[rows_a(1, o)], ra2.at[0, i], A2 + i, at_x(1))
        got(ra1.at[1, i], A1 + 8 + i)
        add(rows_a(-1, o, HA, HA), ra1.at[1, i])
        send(numer.at[rows_a(-1, o)], ra2.at[1, i], A2 + 8 + i, at_x(-1))

    def a2_step(i):
        o = ORDER_RS[i]
        got(ra2.at[0, i], A2 + i)
        got(ra2.at[1, i], A2 + 8 + i)
        numer[rows_a(0, o), :] += ra2[0, i] + ra2[1, i]

    for i in range(4):
        a1_step(i)
    bz_step(2)
    for i in range(4, 8):
        a1_step(i)

    for d in range(1, NX):
        got(rw1.at[d - 1], W1 + d - 1)
    w = wown[x] + rw1[0] + rw1[1] + rw1[2]
    for s in range(NZ):
        w2s[s] = w[s : s + 1, :]
    for d in range(1, NZ):
        send(w2s.at[mod(z + d, NZ)], rw2.at[d - 1], W2 + d - 1, at_z(d))

    bz_step(3)
    a2_step(0)
    send(numer.at[rows_a(0, 4, 0, HA)], raz0.at[0], AZ, at_z(1))
    send(numer.at[rows_a(0, 4, HA, HA)], raz0.at[1], AZ + 4, at_z(-1))

    def az_step(k):
        if k == 1:
            got(raz0.at[0], AZ)
            add(rows_a(0, 3, 0, HA), raz0.at[0])
        else:
            got(raz.at[k - 2, 0], AZ + k - 1)
            add(rows_a(0, 4 - k), raz.at[k - 2, 0])
        send(numer.at[rows_a(0, 4 - k)], raz.at[k - 1, 0], AZ + k, at_z(1))
        if k == 1:
            got(raz0.at[1], AZ + 4)
            add(rows_a(0, -3, HA, HA), raz0.at[1])
        else:
            got(raz.at[k - 2, 1], AZ + 4 + k - 1)
            add(rows_a(0, k - 4), raz.at[k - 2, 1])
        send(numer.at[rows_a(0, k - 4)], raz.at[k - 1, 1], AZ + 4 + k, at_z(-1))

    a2_step(1)
    a2_step(2)
    az_step(1)

    got(rbz.at[2, 0], BZ + 3)
    got(rbz.at[2, 1], BZ + 7)
    numer[chunk_rows_b(0), :] += rbz[2, 0] + rbz[2, 1]
    send(numer.at[rows_b(0, 2, 0, HB)], rbx0.at[0], BX, at_x(1))
    send(numer.at[rows_b(0, 2, HB, HB)], rbx0.at[1], BX + 2, at_x(-1))
    a2_step(3)
    a2_step(4)
    az_step(2)
    got(rbx0.at[0], BX)
    add(rows_b(0, 1, 0, HB), rbx0.at[0])
    send(numer.at[rows_b(0, 1)], rbx.at[0], BX + 1, at_x(1))
    got(rbx0.at[1], BX + 2)
    add(rows_b(0, -1, HB, HB), rbx0.at[1])
    send(numer.at[rows_b(0, -1)], rbx.at[1], BX + 3, at_x(-1))

    w = w2s[z]
    for d in range(1, NZ):
        got(rw2.at[d - 1], W2 + d - 1)
        w = w + rw2[d - 1]
    den[...] = jnp.broadcast_to(w, (RA + RB, RA + RB)).T + PRIOR

    def finish(rows, total_rows, den_rows):
        q = den[den_rows, :]
        q = jnp.concatenate([q, q], axis=1)
        out[rows, :] = (total_rows * (1.0 / XSCALE) + PRIOR * cbuf[rows, :]) / q

    a2_step(5)
    a2_step(6)
    az_step(3)
    got(rbx.at[0], BX + 1)
    got(rbx.at[1], BX + 3)
    own_b = rows_b(0, 0)
    finish(own_b, numer[own_b, :] + rbx[0] + rbx[1], pl.ds(RA, RB))
    send(out.at[own_b], out.at[own_b], GBX, at_x(1))
    send(out.at[own_b], out.at[own_b], GBX + 2, at_x(-1))

    a2_step(7)
    got(raz.at[2, 0], AZ + 3)
    got(raz.at[2, 1], AZ + 7)
    own_a = rows_a(0, 0)
    finish(own_a, numer[own_a, :] + raz[2, 0] + raz[2, 1], pl.ds(0, RA))

    def gaz_send(k):
        if k < 3:
            r, l = rows_a(0, -k), rows_a(0, k)
        else:
            r, l = rows_a(0, -3, 0, HA), rows_a(0, 3, HA, HA)
        send(out.at[r], out.at[r], GAZ + k, at_z(1))
        send(out.at[l], out.at[l], GAZ + 4 + k, at_z(-1))

    def gaz_got(k):
        if k < 3:
            r, l = rows_a(0, -1 - k), rows_a(0, 1 + k)
        else:
            r, l = rows_a(0, 4, 0, HA), rows_a(0, 4, HA, HA)
        got(out.at[r], GAZ + k)
        got(out.at[l], GAZ + 4 + k)

    def ga1_send(i):
        r = rows_a(0, ORDER_AG[i])
        send(out.at[r], out.at[r], GA1 + i, at_x(1))
        send(out.at[r], out.at[r], GA1 + 8 + i, at_x(-1))

    def ga2_step(i):
        o = ORDER_AG[i]
        got(out.at[rows_a(-1, o)], GA1 + i)
        r = rows_a(-1, o, 0, HA)
        send(out.at[r], out.at[r], GA2 + i, at_x(1))
        got(out.at[rows_a(1, o)], GA1 + 8 + i)
        l = rows_a(1, o, HA, HA)
        send(out.at[l], out.at[l], GA2 + 8 + i, at_x(-1))

    def ga2_got(i):
        o = ORDER_AG[i]
        got(out.at[rows_a(2, o, 0, HA)], GA2 + i)
        got(out.at[rows_a(2, o, HA, HA)], GA2 + 8 + i)

    def gbz_send(k):
        if k < 3:
            r, l = chunk_rows_b(-k), chunk_rows_b(k)
        else:
            r, l = chunk_rows_b(-3, 0, HC), chunk_rows_b(3, HC, HC)
        send(out.at[r], out.at[r], GBZ + k, at_z(1))
        send(out.at[l], out.at[l], GBZ + 4 + k, at_z(-1))

    def gbz_got(k):
        if k < 3:
            r, l = chunk_rows_b(-1 - k), chunk_rows_b(1 + k)
        else:
            r, l = chunk_rows_b(4, 0, HC), chunk_rows_b(4, HC, HC)
        got(out.at[r], GBZ + k)
        got(out.at[l], GBZ + 4 + k)

    gaz_send(0)
    ga1_send(0)
    got(out.at[rows_b(0, -1)], GBX)
    r = rows_b(0, -1, 0, HB)
    send(out.at[r], out.at[r], GBX + 1, at_x(1))
    got(out.at[rows_b(0, 1)], GBX + 2)
    l = rows_b(0, 1, HB, HB)
    send(out.at[l], out.at[l], GBX + 3, at_x(-1))
    gaz_got(0)
    gaz_send(1)
    ga1_send(1)
    ga1_send(2)
    got(out.at[rows_b(0, 2, 0, HB)], GBX + 1)
    got(out.at[rows_b(0, 2, HB, HB)], GBX + 3)
    gbz_send(0)
    gaz_got(1)
    gaz_send(2)
    ga1_send(3)
    ga1_send(4)
    ga2_step(0)
    gaz_got(2)
    gaz_send(3)
    ga1_send(5)
    ga1_send(6)
    gbz_got(0)
    gbz_send(1)
    gaz_got(3)
    ga1_send(7)
    ga2_step(1)
    ga2_step(2)
    gbz_got(1)
    gbz_send(2)
    ga2_step(3)
    ga2_step(4)
    gbz_got(2)
    gbz_send(3)
    ga2_step(5)
    ga2_step(6)
    ga2_step(7)
    gbz_got(3)
    for i in range(8):
        ga2_got(i)
    for c in pending:
        c.wait_send()


def local(vectors, centroids):
    f32, bf16 = jnp.float32, jnp.bfloat16
    V = pltpu.VMEM
    refined, lse = pl.pallas_call(
        kernel,
        out_shape=(
            jax.ShapeDtypeStruct((KP, D), f32),
            jax.ShapeDtypeStruct((1, N), f32),
        ),
        in_specs=[pl.BlockSpec(memory_space=pl.ANY)] * 2,
        out_specs=[pl.BlockSpec(memory_space=pltpu.VMEM)] * 2,
        scratch_shapes=[
            V((N, D), f32), V((KP, D), f32),
            V((N, D), bf16), V((N, D), bf16), V((D, N), bf16), V((D, N), bf16),
            V((KP, N), f32), V((NT, 8, N), f32), V((NT, 8, N), f32), V((NT, 8, N), f32),
            V((NC, 1, N), f32), V((KP, D), f32), V((KP, 128), f32),
            V((NX, NZ, 128), f32), V((NX - 1, NZ, 128), f32),
            V((NZ, 1, 128), f32), V((NZ - 1, 1, 128), f32),
            V((2, 8, RA // 2, D), f32), V((2, 8, RA, D), f32),
            V((2, RA // 2, D), f32), V((3, 2, RA, D), f32),
            V((2, CB // 2, D), f32), V((3, 2, CB, D), f32),
            V((2, RB // 2, D), f32), V((2, RB, D), f32),
            V((RA + RB, RA + RB), f32),
            pltpu.SemaphoreType.DMA((NSEM,)), pltpu.SemaphoreType.DMA((NSEM,)),
            pltpu.SemaphoreType.DMA((NT + 1,)),
        ],
        compiler_params=pltpu.CompilerParams(
            collective_id=0, has_side_effects=True, vmem_limit_bytes=58 * 1024 * 1024
        ),
    )(vectors, centroids)
    return refined, lse.reshape(N)


def solution(mesh):
    return jax.shard_map(
        local,
        mesh=mesh,
        in_specs=(P("item", None), P("cent", None)),
        out_specs=(P("cent", None), P("item")),
        check_vma=False,
    )
```

```python
import functools
import math

import jax
import jax.numpy as jnp
from jax import lax
from jax.experimental import pallas as pl
from jax.experimental.pallas import tpu as pltpu
from jax.sharding import PartitionSpec as P

MESH = pl.DeviceIdType.MESH
BOLTZMANN_SCALE = 8.0
PRIOR = 2.0
LOG2E = math.log2(math.e)
LN2 = math.log(2.0)
XSCALE = 2.0 * LOG2E / BOLTZMANN_SCALE

NX, NZ, NC = 4, 8, 8
D = 256
N = 1024
KP = 4096
RA, RB = 80, 48
CA, CB = NZ * RA, NX * RB
B0 = NX * CA
TB = 768
NTB = NZ * CB // TB
NT = NX + NTB
Q = 2

STAT = 0
W1 = STAT + 7
W2 = W1 + 3
A1 = W2 + 7
A2 = A1 + 16
AZ = A2 + 16
BZ = AZ + 8
BX = BZ + 8 * Q
GAZ = BX + 3
GA1 = GAZ + 8
GA2 = GA1 + 16
GBX = GA2 + 16
GBZ = GBX + 3
NSEM = GBZ + 32

ORDER_RS = (4, 3, -3, 2, -2, 1, -1, 0)
ORDER_AG = (0, -1, 1, -2, 2, -3, 3, 4)
ORDER_T = (0, -1, 1, 2)


def dot(a, b):
    return jnp.dot(a, b, preferred_element_type=jnp.float32)


def split(v):
    hi = v.astype(jnp.bfloat16)
    lo = (v - hi.astype(jnp.float32)).astype(jnp.bfloat16)
    return hi, lo


def kernel(
    x_hbm, c_hbm, out, lse_out,
    xbuf, cbuf, xh, xl, xht, xlt, e_buf, m_buf, s_buf, f_buf, stat, numer, w8,
    wown, rw1, w2s, rw2, ra1, ra2, raz0, raz, rbz0, rbz, rbx, den,
    ss, rs, lsem,
):
    item = lax.axis_index("item")
    cent = lax.axis_index("cent")
    x, z = item // NZ, lax.rem(item, NZ)

    def mod(v, n):
        return lax.rem(v + 2 * n, n)

    def at_x(d):
        return {"item": mod(x + d, NX) * NZ + z}

    def at_z(d):
        return {"item": x * NZ + mod(z + d, NZ)}

    def at_c(d):
        return {"cent": mod(cent + d, NC)}

    pending = []

    def copy(src, dst, k, dev):
        return pltpu.make_async_remote_copy(
            src_ref=src, dst_ref=dst, send_sem=ss.at[k], recv_sem=rs.at[k],
            device_id=dev, device_id_type=MESH,
        )

    def send(make):
        make().start()
        pending.append(make)

    def got(region, k):
        copy(region, region, k, at_x(1)).wait_recv()

    x_load = pltpu.make_async_copy(x_hbm, xbuf, lsem.at[NT])
    x_load.start()

    def tile_rows(t, rows_n, base):
        return pl.ds(pl.multiple_of(base + t * rows_n, 8), rows_n)

    def c_load(t, rows_n, base, k):
        rows = tile_rows(t, rows_n, base)
        return pltpu.make_async_copy(c_hbm.at[rows], cbuf.at[rows], lsem.at[k])

    for t in range(NX):
        c_load(t, CA, 0, t).start()
    for t in range(NTB):
        c_load(t, TB, B0, NX + t).start()

    barrier = pltpu.get_barrier_semaphore()
    for d in range(1, NX):
        pl.semaphore_signal(barrier, inc=1, device_id=at_x(d), device_id_type=MESH)
    for d in range(1, NZ):
        pl.semaphore_signal(barrier, inc=1, device_id=at_z(d), device_id_type=MESH)
    for d in range(1, NC):
        pl.semaphore_signal(barrier, inc=1, device_id=at_c(d), device_id_type=MESH)

    x_load.wait()
    for j in range(N // 256):
        rows = pl.ds(j * 256, 256)
        v = xbuf[rows, :] * XSCALE
        hi, lo = split(v)
        xh[rows, :] = hi
        xl[rows, :] = lo
        hi, lo = split(v.T)
        xht[:, rows] = hi
        xlt[:, rows] = lo

    def stage_a(rows_n, base, first):
        def tile(t, _):
            c_load(t, rows_n, base, first + t).wait()
            rows = tile_rows(t, rows_n, base)
            c = cbuf[rows, :]
            csq = jnp.sum(c * c, axis=1, keepdims=True) * (LOG2E / BOLTZMANN_SCALE)
            ch, cl = split(c)
            for j in range(N // 256):
                cols = pl.ds(j * 256, 256)
                b = xht[:, cols]
                l = dot(ch, b) + dot(cl, b) + dot(ch, xlt[:, cols]) - csq
                l = l.reshape(rows_n // 8, 8, 256)
                m = jnp.max(l, axis=0)
                e = jnp.exp2(l - m[None])
                e_buf[rows, cols] = e.reshape(rows_n, 256)
                m_buf[first + t, :, cols] = m
                s_buf[first + t, :, cols] = jnp.sum(e, axis=0)
            return 0

        return tile

    lax.fori_loop(0, NX, stage_a(CA, 0, 0), 0)
    lax.fori_loop(0, NTB, stage_a(TB, B0, NX), 0)

    mm = m_buf[...]
    m_loc = jnp.max(jnp.max(mm, axis=0), axis=0, keepdims=True)
    s_loc = jnp.sum(
        jnp.sum(s_buf[...] * jnp.exp2(mm - m_loc[None]), axis=0), axis=0, keepdims=True
    )
    stat[cent] = m_loc + jnp.log(s_loc) * LOG2E
    pl.semaphore_wait(barrier, (NX - 1) + (NZ - 1) + (NC - 1))
    for d in range(1, NC):
        send(lambda d=d: copy(stat.at[cent], stat.at[cent], STAT + d - 1, at_c(d)))
    for d in range(1, NC):
        got(stat.at[mod(cent - d, NC)], STAT + d - 1)
    parts = stat[...]
    top = jnp.max(parts, axis=0)
    total = jnp.log(jnp.sum(jnp.exp2(parts - top[None]), axis=0))
    lse_out[...] = (top * LN2 + total).reshape(N)
    lse2 = top + total * LOG2E
    f_buf[...] = jnp.exp2(mm - lse2[None])

    def block_b(pieces, f):
        hs, ls = [], []
        for rows in pieces:
            n = rows.size
            p = (e_buf[rows, :].reshape(n // 8, 8, N) * f[None]).reshape(n, N)
            w = p[:, 0:128]
            for q in range(1, N // 128):
                w = w + p[:, q * 128 : (q + 1) * 128]
            w8[rows, :] = w
            hi, lo = split(p)
            hs.append(hi)
            ls.append(lo)
        hi = jnp.concatenate(hs, axis=0)
        lo = jnp.concatenate(ls, axis=0)
        r = dot(hi, xh[...]) + dot(lo, xh[...]) + dot(hi, xl[...])
        at = 0
        for rows in pieces:
            numer[rows, :] = r[at : at + rows.size]
            at += rows.size

    def rows_a(dx, dz, off=0, n=RA):
        return pl.ds(pl.multiple_of(mod(x + dx, NX) * CA + mod(z + dz, NZ) * RA + off, 8), n)

    def rows_b(dz, dx, off=0, n=RB):
        return pl.ds(pl.multiple_of(B0 + mod(z + dz, NZ) * CB + mod(x + dx, NX) * RB + off, 8), n)

    def chunk_rows_b(dz, off=0, n=CB):
        return pl.ds(pl.multiple_of(B0 + mod(z + dz, NZ) * CB + off, 8), n)

    def add(rows, ref):
        numer[rows, :] += ref[...]

    HA, HB = RA // 2, RB // 2
    CQ = CB // Q
    HQ = CQ // 2

    def a1_send(i):
        o = ORDER_RS[i]
        send(lambda: copy(numer.at[rows_a(2, o, 0, HA)], ra1.at[0, i], A1 + i, at_x(1)))
        send(lambda: copy(numer.at[rows_a(2, o, HA, HA)], ra1.at[1, i], A1 + 8 + i, at_x(-1)))

    def a1_step(i):
        o = ORDER_RS[i]
        got(ra1.at[0, i], A1 + i)
        add(rows_a(1, o, 0, HA), ra1.at[0, i])
        send(lambda: copy(numer.at[rows_a(1, o)], ra2.at[0, i], A2 + i, at_x(1)))
        got(ra1.at[1, i], A1 + 8 + i)
        add(rows_a(-1, o, HA, HA), ra1.at[1, i])
        send(lambda: copy(numer.at[rows_a(-1, o)], ra2.at[1, i], A2 + 8 + i, at_x(-1)))

    def a2_step(i):
        o = ORDER_RS[i]
        got(ra2.at[0, i], A2 + i)
        got(ra2.at[1, i], A2 + 8 + i)
        numer[rows_a(0, o), :] += ra2[0, i] + ra2[1, i]

    def az_send0():
        send(lambda: copy(numer.at[rows_a(0, 4, 0, HA)], raz0.at[0], AZ, at_z(1)))
        send(lambda: copy(numer.at[rows_a(0, 4, HA, HA)], raz0.at[1], AZ + 4, at_z(-1)))

    def az_step(k):
        for e, sg in ((0, 1), (1, -1)):
            sem = AZ + 4 * e
            if k == 1:
                got(raz0.at[e], sem)
                add(rows_a(0, 3 * sg, e * HA, HA), raz0.at[e])
            else:
                got(raz.at[k - 2, e], sem + k - 1)
                add(rows_a(0, (4 - k) * sg), raz.at[k - 2, e])
            send(lambda e=e, sg=sg, sem=sem: copy(
                numer.at[rows_a(0, (4 - k) * sg)], raz.at[k - 1, e], sem + k, at_z(sg)))

    def bz_send0(q):
        for e, sg in ((0, 1), (1, -1)):
            send(lambda e=e, sg=sg: copy(
                numer.at[chunk_rows_b(4, q * CQ + e * HQ, HQ)], rbz0.at[e, q],
                BZ + 8 * q + 4 * e, at_z(sg)))

    def bz_step(k, q):
        for e, sg in ((0, 1), (1, -1)):
            sem = BZ + 8 * q + 4 * e
            if k == 1:
                got(rbz0.at[e, q], sem)
                add(chunk_rows_b(3 * sg, q * CQ + e * HQ, HQ), rbz0.at[e, q])
            else:
                got(rbz.at[k - 2, e, q], sem + k - 1)
                add(chunk_rows_b((4 - k) * sg, q * CQ, CQ), rbz.at[k - 2, e, q])
            send(lambda e=e, sg=sg, sem=sem: copy(
                numer.at[chunk_rows_b((4 - k) * sg, q * CQ, CQ)], rbz.at[k - 1, e, q],
                sem + k, at_z(sg)))

    def bz_last(q):
        got(rbz.at[2, 0, q], BZ + 8 * q + 3)
        got(rbz.at[2, 1, q], BZ + 8 * q + 7)
        numer[chunk_rows_b(0, q * CQ, CQ), :] += rbz[2, 0, q] + rbz[2, 1, q]

    def blocks(j, _):
        late = j // 6
        r = lax.rem(j, 3)
        dx = (2 - r - r // 2) * (1 - late)
        h = (j // 3) * (1 - late) + (j - 6) * late
        pieces = [rows_a(dx, 4 - 6 * h), rows_a(dx, 3 - 2 * h), rows_a(dx, 2 * h - 3), rows_a(dx, 2 - 2 * h)]
        block_b(pieces, f_buf[mod(x + dx, NX)])

        @pl.when(j == 0)
        def _():
            for i in range(4):
                a1_send(i)

        @pl.when(j == 3)
        def _():
            for i in range(4, 8):
                a1_send(i)

        dz = 4 + (1 - 2 * lax.rem(j, 2)) * ((j + 1) // 2)
        block_b([chunk_rows_b(dz)], f_buf[NX + mod(z + dz, NZ) // (NZ // NTB)])

        @pl.when(j == 0)
        def _():
            bz_send0(0)
            bz_send0(1)

        @pl.when(j == 2)
        def _():
            a1_step(0)

        @pl.when(j == 3)
        def _():
            bz_step(1, 0)
            bz_step(1, 1)
            a1_step(1)

        @pl.when(j == 4)
        def _():
            a1_step(2)
            a1_step(3)

        @pl.when(j == 6)
        def _():
            a1_step(4)
            a1_step(5)

        return 0

    lax.fori_loop(0, 8, blocks, 0)
    a1_step(6)
    a1_step(7)

    def owner_weights(i, _):
        xd, zd = i // NZ, lax.rem(i, NZ)
        a = w8[pl.ds(pl.multiple_of(xd * CA + zd * RA, 8), RA), :]
        b = w8[pl.ds(pl.multiple_of(B0 + zd * CB + xd * RB, 8), RB), :]
        t = jnp.concatenate([a, b], axis=0).T
        wown[xd, pl.ds(zd, 1), :] = jnp.sum(t, axis=0, keepdims=True)
        return 0

    a2_step(0)
    az_send0()
    bz_step(2, 0)
    lax.fori_loop(0, 8, owner_weights, 0)
    bz_step(2, 1)
    lax.fori_loop(8, 20, owner_weights, 0)
    a2_step(1)
    a2_step(2)
    az_step(1)
    lax.fori_loop(20, 32, owner_weights, 0)
    for d in range(1, NX):
        send(lambda d=d: copy(wown.at[mod(x + d, NX)], rw1.at[d - 1], W1 + d - 1, at_x(d)))
    bz_step(3, 0)
    a2_step(3)
    bz_step(3, 1)
    a2_step(4)
    az_step(2)

    for d in range(1, NX):
        got(rw1.at[d - 1], W1 + d - 1)
    w = wown[x] + rw1[0] + rw1[1] + rw1[2]
    for s in range(NZ):
        w2s[s] = w[s : s + 1, :]
    for d in range(1, NZ):
        send(lambda d=d: copy(w2s.at[mod(z + d, NZ)], rw2.at[d - 1], W2 + d - 1, at_z(d)))

    bz_last(0)
    a2_step(5)
    bz_last(1)
    for d in range(1, NX):
        send(lambda d=d: copy(numer.at[rows_b(0, d)], rbx.at[d - 1], BX + d - 1, at_x(d)))
    a2_step(6)
    az_step(3)
    a2_step(7)

    w = w2s[z]
    for d in range(1, NZ):
        got(rw2.at[d - 1], W2 + d - 1)
        w = w + rw2[d - 1]
    den[...] = jnp.broadcast_to(w, (RA + RB, RA + RB)).T + PRIOR

    def finish(rows, total_rows, den_rows):
        q = den[den_rows, :]
        q = jnp.concatenate([q, q], axis=1)
        out[rows, :] = (total_rows * (1.0 / XSCALE) + PRIOR * cbuf[rows, :]) / q

    def give(rows, k, dev):
        send(lambda: copy(out.at[rows()], out.at[rows()], k, dev()))

    def gaz_send(k):
        for e, sg in ((0, 1), (1, -1)):
            if k < 3:
                rows = lambda sg=sg: rows_a(0, -k * sg)
            else:
                rows = lambda e=e, sg=sg: rows_a(0, -3 * sg, e * HA, HA)
            give(rows, GAZ + 4 * e + k, lambda sg=sg: at_z(sg))

    def gaz_got(k):
        for e, sg in ((0, 1), (1, -1)):
            r = rows_a(0, -(1 + k) * sg) if k < 3 else rows_a(0, 4, e * HA, HA)
            got(out.at[r], GAZ + 4 * e + k)

    def ga1_send(i):
        give(lambda: rows_a(0, ORDER_AG[i]), GA1 + i, lambda: at_x(1))
        give(lambda: rows_a(0, ORDER_AG[i]), GA1 + 8 + i, lambda: at_x(-1))

    def ga2_send(i):
        give(lambda: rows_a(0, ORDER_AG[i]), GA2 + i, lambda: at_x(2))

    def ga1_got(i):
        got(out.at[rows_a(-1, ORDER_AG[i])], GA1 + i)
        got(out.at[rows_a(1, ORDER_AG[i])], GA1 + 8 + i)

    def ga2_step(i):
        o = ORDER_AG[i]
        got(out.at[rows_a(-1, o)], GA1 + i)
        give(lambda: rows_a(-1, o, 0, HA), GA2 + i, lambda: at_x(1))
        got(out.at[rows_a(1, o)], GA1 + 8 + i)
        give(lambda: rows_a(1, o, HA, HA), GA2 + 8 + i, lambda: at_x(-1))

    def ga2_got(i):
        o = ORDER_AG[i]
        got(out.at[rows_a(2, o, 0, HA)], GA2 + i)
        got(out.at[rows_a(2, o, HA, HA)], GA2 + 8 + i)

    def gbz_send(k, j):
        t = ORDER_T[j]
        for e, sg in ((0, 1), (1, -1)):
            if k < 3:
                rows = lambda sg=sg: rows_b(-k * sg, t)
            else:
                rows = lambda e=e, sg=sg: rows_b(-3 * sg, t, e * HB, HB)
            give(rows, GBZ + 8 * j + 4 * e + k, lambda sg=sg: at_z(sg))

    def gbz_got(k, j):
        t = ORDER_T[j]
        for e, sg in ((0, 1), (1, -1)):
            r = rows_b(-(1 + k) * sg, t) if k < 3 else rows_b(4, t, e * HB, HB)
            got(out.at[r], GBZ + 8 * j + 4 * e + k)

    def gbz_step(k, j):
        gbz_got(k, j)
        gbz_send(k + 1, j)

    for d in range(1, NX):
        got(rbx.at[d - 1], BX + d - 1)
    own_b = rows_b(0, 0)
    finish(own_b, numer[own_b, :] + rbx[0] + rbx[1] + rbx[2], pl.ds(RA, RB))
    for d in (2, 1, 3):
        give(lambda: rows_b(0, 0), GBX + d - 1, lambda d=d: at_x(d))
    gbz_send(0, 0)

    got(raz.at[2, 0], AZ + 3)
    got(raz.at[2, 1], AZ + 7)
    own_a = rows_a(0, 0)
    finish(own_a, numer[own_a, :] + raz[2, 0] + raz[2, 1], pl.ds(0, RA))
    gaz_send(0)
    ga1_send(0)

    for d in (1, 3, 2):
        got(out.at[rows_b(0, -d)], GBX + d - 1)
        gbz_send(0, (0, 1, 3, 2)[d])
    gbz_step(0, 0)
    gaz_got(0)
    gaz_send(1)
    ga1_send(1)
    ga1_send(2)
    for j in (1, 2, 3):
        gbz_step(0, j)
    ga2_step(0)
    gbz_step(1, 0)
    gaz_got(1)
    gaz_send(2)
    ga1_send(3)
    ga1_send(4)
    ga2_step(1)
    ga2_step(2)
    for j in (1, 2, 3):
        gbz_step(1, j)
    gbz_step(2, 0)
    gaz_got(2)
    gaz_send(3)
    ga1_send(5)
    ga1_send(6)
    ga2_step(3)
    ga2_step(4)
    gaz_got(3)
    ga1_send(7)
    ga2_send(7)
    for j in (1, 2, 3):
        gbz_step(2, j)
    ga2_step(5)
    ga2_step(6)
    for j in range(4):
        gbz_got(3, j)
    for i in range(7):
        ga2_got(i)
    ga1_got(7)
    got(out.at[rows_a(2, ORDER_AG[7])], GA2 + 7)
    for make in pending:
        make().wait_send()


def local(vectors, centroids):
    f32, bf16 = jnp.float32, jnp.bfloat16
    V = pltpu.VMEM
    refined, lse = pl.pallas_call(
        kernel,
        out_shape=(
            V((KP, D), f32),
            V((N,), f32),
        ),
        in_specs=[pl.BlockSpec(memory_space=pl.ANY)] * 2,
        out_specs=[pl.BlockSpec(memory_space=pltpu.VMEM)] * 2,
        scratch_shapes=[
            V((N, D), f32), V((KP, D), f32),
            V((N, D), bf16), V((N, D), bf16), V((D, N), bf16), V((D, N), bf16),
            V((KP, N), f32), V((NT, 8, N), f32), V((NT, 8, N), f32), V((NT, 8, N), f32),
            V((NC, 1, N), f32), V((KP, D), f32), V((KP, 128), f32),
            V((NX, NZ, 128), f32), V((NX - 1, NZ, 128), f32),
            V((NZ, 1, 128), f32), V((NZ - 1, 1, 128), f32),
            V((2, 8, RA // 2, D), f32), V((2, 8, RA, D), f32),
            V((2, RA // 2, D), f32), V((3, 2, RA, D), f32),
            V((2, Q, CB // Q // 2, D), f32), V((3, 2, Q, CB // Q, D), f32),
            V((NX - 1, RB, D), f32),
            V((RA + RB, RA + RB), f32),
            pltpu.SemaphoreType.DMA((NSEM,)), pltpu.SemaphoreType.DMA((NSEM,)),
            pltpu.SemaphoreType.DMA((NT + 1,)),
        ],
        compiler_params=pltpu.CompilerParams(
            collective_id=0, has_side_effects=True, vmem_limit_bytes=50 * 1024 * 1024
        ),
    )(vectors, centroids)
    return refined, lse


def solution(mesh):
    return jax.shard_map(
        local,
        mesh=mesh,
        in_specs=(P("item", None), P("cent", None)),
        out_specs=(P("cent", None), P("item")),
        check_vma=False,
    )
```

```python
import functools
import math

import jax
import jax.numpy as jnp
from jax import lax
from jax.experimental import pallas as pl
from jax.experimental.pallas import tpu as pltpu
from jax.sharding import PartitionSpec as P

MESH = pl.DeviceIdType.MESH
BOLTZMANN_SCALE = 8.0
PRIOR = 2.0
LOG2E = math.log2(math.e)
LN2 = math.log(2.0)
XSCALE = 2.0 * LOG2E / BOLTZMANN_SCALE

NX, NZ, NC = 4, 8, 8
D = 256
N = 1024
KP = 4096
RA, RB = 80, 48
CA, CB = NZ * RA, NX * RB
B0 = NX * CA
TB = 768
NTB = NZ * CB // TB
NT = NX + NTB
Q = 2

STAT, W1, W2, BX, GBX = range(5)
A1 = 5
A2 = A1 + 8
AZ = A2 + 8
BZ = AZ + 4
GAZ = BZ + 4 * Q
GA1 = GAZ + 4
GA2 = GA1 + 8
GBZ = GA2 + 8
NRECV = GBZ + 16
S_STAT, S_W1, S_W2, S_BX, S_GBX, S_A1, S_A2, S_AZ, S_BZ, S_GAZ, S_GA1, S_GA2, S_GBZ = range(13)
NSEND = 13

ORDER_RS = (4, 3, -3, 2, -2, 1, -1, 0)
ORDER_AG = (0, -1, 1, -2, 2, -3, 3, 4)
ORDER_T = (0, -1, 1, 2)


def dot(a, b):
    return jnp.dot(a, b, preferred_element_type=jnp.float32)


def split(v):
    hi = v.astype(jnp.bfloat16)
    lo = (v - hi.astype(jnp.float32)).astype(jnp.bfloat16)
    return hi, lo


def kernel(
    x_hbm, c_hbm, out, lse_out,
    xbuf, cbuf, xh, xl, xht, xlt, e_buf, m_buf, s_buf, f_buf, stat, numer, w8,
    wown, rw1, w2s, rw2, ra1, ra2, raz0, raz, rbz0, rbz, rbx, den,
    ss, rs, lsem,
):
    item = lax.axis_index("item")
    cent = lax.axis_index("cent")
    x, z = item // NZ, lax.rem(item, NZ)

    def mod(v, n):
        return lax.rem(v + 2 * n, n)

    def at_x(d):
        return {"item": mod(x + d, NX) * NZ + z}

    def at_z(d):
        return {"item": x * NZ + mod(z + d, NZ)}

    def at_c(d):
        return {"cent": mod(cent + d, NC)}

    def copy(src, dst, kind, k, dev):
        return pltpu.make_async_remote_copy(
            src_ref=src, dst_ref=dst, send_sem=ss.at[kind], recv_sem=rs.at[k],
            device_id=dev, device_id_type=MESH,
        )

    def send(src, dst, kind, k, dev):
        copy(src, dst, kind, k, dev).start()

    def got(region, k):
        copy(region, region, 0, k, at_x(1)).wait_recv()

    def sent(region, kind):
        copy(region, region, kind, 0, at_x(1)).wait_send()

    def x_load(j):
        rows = pl.ds(j * 256, 256)
        return pltpu.make_async_copy(x_hbm.at[rows], xbuf.at[rows], lsem.at[NT + j])

    for j in range(N // 256):
        x_load(j).start()

    def tile_rows(t, rows_n, base):
        return pl.ds(pl.multiple_of(base + t * rows_n, 8), rows_n)

    def c_load(t, rows_n, base, k):
        rows = tile_rows(t, rows_n, base)
        return pltpu.make_async_copy(c_hbm.at[rows], cbuf.at[rows], lsem.at[k])

    for t in range(NX):
        c_load(t, CA, 0, t).start()
    for t in range(NTB):
        c_load(t, TB, B0, NX + t).start()

    barrier = pltpu.get_barrier_semaphore()
    for d in range(1, NX):
        pl.semaphore_signal(barrier, inc=1, device_id=at_x(d), device_id_type=MESH)
    for d in range(1, NZ):
        pl.semaphore_signal(barrier, inc=1, device_id=at_z(d), device_id_type=MESH)
    for d in range(1, NC):
        pl.semaphore_signal(barrier, inc=1, device_id=at_c(d), device_id_type=MESH)

    for j in range(N // 256):
        x_load(j).wait()
        rows = pl.ds(j * 256, 256)
        v = xbuf[rows, :] * XSCALE
        hi, lo = split(v)
        xh[rows, :] = hi
        xl[rows, :] = lo
        hi, lo = split(v.T)
        xht[:, rows] = hi
        xlt[:, rows] = lo

    def stage_a(rows_n, base, first):
        def tile(t, _):
            c_load(t, rows_n, base, first + t).wait()
            rows = tile_rows(t, rows_n, base)
            c = cbuf[rows, :]
            csq = jnp.sum(c * c, axis=1, keepdims=True) * (LOG2E / BOLTZMANN_SCALE)
            ch, cl = split(c)
            for j in range(N // 256):
                cols = pl.ds(j * 256, 256)
                b = xht[:, cols]
                l = dot(ch, b) + dot(cl, b) + dot(ch, xlt[:, cols]) - csq
                l = l.reshape(rows_n // 8, 8, 256)
                m = jnp.max(l, axis=0)
                e = jnp.exp2(l - m[None])
                e_buf[rows, cols] = e.reshape(rows_n, 256)
                m_buf[first + t, :, cols] = m
                s_buf[first + t, :, cols] = jnp.sum(e, axis=0)
            return 0

        return tile

    lax.fori_loop(0, NX, stage_a(CA, 0, 0), 0)
    lax.fori_loop(0, NTB, stage_a(TB, B0, NX), 0)

    mm = m_buf[...]
    m_loc = jnp.max(jnp.max(mm, axis=0), axis=0, keepdims=True)
    s_loc = jnp.sum(
        jnp.sum(s_buf[...] * jnp.exp2(mm - m_loc[None]), axis=0), axis=0, keepdims=True
    )
    stat[cent] = m_loc + jnp.log(s_loc) * LOG2E
    pl.semaphore_wait(barrier, (NX - 1) + (NZ - 1) + (NC - 1))
    for d in range(1, NC):
        send(stat.at[cent], stat.at[cent], S_STAT, STAT, at_c(d))
    got(stat.at[pl.ds(0, NC - 1)], STAT)
    parts = stat[...]
    top = jnp.max(parts, axis=0)
    total = jnp.log(jnp.sum(jnp.exp2(parts - top[None]), axis=0))
    lse_out[...] = (top * LN2 + total).reshape(N)
    lse2 = top + total * LOG2E
    f_buf[...] = jnp.exp2(mm - lse2[None])

    def block_b(pieces, f):
        hs, ls = [], []
        for rows in pieces:
            n = rows.size
            p = (e_buf[rows, :].reshape(n // 8, 8, N) * f[None]).reshape(n, N)
            w = p[:, 0:128]
            for q in range(1, N // 128):
                w = w + p[:, q * 128 : (q + 1) * 128]
            w8[rows, :] = w
            hi, lo = split(p)
            hs.append(hi)
            ls.append(lo)
        hi = jnp.concatenate(hs, axis=0)
        lo = jnp.concatenate(ls, axis=0)
        r = dot(hi, xh[...]) + dot(lo, xh[...]) + dot(hi, xl[...])
        at = 0
        for rows in pieces:
            numer[rows, :] = r[at : at + rows.size]
            at += rows.size

    def rows_a(dx, dz, off=0, n=RA):
        return pl.ds(pl.multiple_of(mod(x + dx, NX) * CA + mod(z + dz, NZ) * RA + off, 8), n)

    def rows_b(dz, dx, off=0, n=RB):
        return pl.ds(pl.multiple_of(B0 + mod(z + dz, NZ) * CB + mod(x + dx, NX) * RB + off, 8), n)

    def chunk_rows_b(dz, off=0, n=CB):
        return pl.ds(pl.multiple_of(B0 + mod(z + dz, NZ) * CB + off, 8), n)

    def add(rows, ref):
        numer[rows, :] += ref[...]

    HA, HB = RA // 2, RB // 2
    CQ = CB // Q
    HQ = CQ // 2

    SIDES = ((0, 1), (1, -1))

    def a1_send(i):
        for e, sg in SIDES:
            send(numer.at[rows_a(2, ORDER_RS[i], e * HA, HA)], ra1.at[i, e], S_A1, A1 + i, at_x(sg))

    def a1_step(i):
        o = ORDER_RS[i]
        got(ra1.at[i], A1 + i)
        for e, sg in SIDES:
            add(rows_a(sg, o, e * HA, HA), ra1.at[i, e])
            send(numer.at[rows_a(sg, o)], ra2.at[i, e], S_A2, A2 + i, at_x(sg))

    def a2_step(i):
        got(ra2.at[i], A2 + i)
        numer[rows_a(0, ORDER_RS[i]), :] += ra2[i, 0] + ra2[i, 1]

    def az_send0():
        for e, sg in SIDES:
            send(numer.at[rows_a(0, 4, e * HA, HA)], raz0.at[e], S_AZ, AZ, at_z(sg))

    def az_step(k):
        got(raz0 if k == 1 else raz.at[k - 2], AZ + k - 1)
        for e, sg in SIDES:
            if k == 1:
                add(rows_a(0, 3 * sg, e * HA, HA), raz0.at[e])
            else:
                add(rows_a(0, (4 - k) * sg), raz.at[k - 2, e])
            send(numer.at[rows_a(0, (4 - k) * sg)], raz.at[k - 1, e], S_AZ, AZ + k, at_z(sg))

    def bz_send0(q):
        for e, sg in SIDES:
            send(
                numer.at[chunk_rows_b(4, q * CQ + e * HQ, HQ)], rbz0.at[q, e],
                S_BZ, BZ + 4 * q, at_z(sg))

    def bz_step(k, q):
        got(rbz0.at[q] if k == 1 else rbz.at[k - 2, q], BZ + 4 * q + k - 1)
        for e, sg in SIDES:
            if k == 1:
                add(chunk_rows_b(3 * sg, q * CQ + e * HQ, HQ), rbz0.at[q, e])
            else:
                add(chunk_rows_b((4 - k) * sg, q * CQ, CQ), rbz.at[k - 2, q, e])
            send(
                numer.at[chunk_rows_b((4 - k) * sg, q * CQ, CQ)], rbz.at[k - 1, q, e],
                S_BZ, BZ + 4 * q + k, at_z(sg))

    def bz_last(q):
        got(rbz.at[2, q], BZ + 4 * q + 3)
        numer[chunk_rows_b(0, q * CQ, CQ), :] += rbz[2, q, 0] + rbz[2, q, 1]

    def owner_weights(i, _):
        xd, zd = i // NZ, lax.rem(i, NZ)
        a = w8[pl.ds(pl.multiple_of(xd * CA + zd * RA, 8), RA), :]
        b = w8[pl.ds(pl.multiple_of(B0 + zd * CB + xd * RB, 8), RB), :]
        t = jnp.concatenate([a, b], axis=0).T
        wown[xd, pl.ds(zd, 1), :] = jnp.sum(t, axis=0, keepdims=True)
        return 0

    def weights(k):
        lax.fori_loop(8 * k, 8 * k + 8, owner_weights, 0)

    def weights_x():
        for d in range(1, NX):
            send(wown.at[mod(x + d, NX)], rw1.at[d - 1], S_W1, W1, at_x(d))

    def weights_z():
        got(rw1, W1)
        w = wown[x] + rw1[0] + rw1[1] + rw1[2]
        for s in range(NZ):
            w2s[s] = w[s : s + 1, :]
        for d in range(1, NZ):
            send(w2s.at[mod(z + d, NZ)], rw2.at[d - 1], S_W2, W2, at_z(d))

    def weights_own():
        got(rw2, W2)
        w = w2s[z]
        for d in range(1, NZ):
            w = w + rw2[d - 1]
        den[...] = jnp.broadcast_to(w, (RA + RB, RA + RB)).T + PRIOR

    def bx_send():
        for d in range(1, NX):
            send(numer.at[rows_b(0, d)], rbx.at[d - 1], S_BX, BX, at_x(d))

    def finish(mine, rows, total_rows):
        q = den[mine, :]
        q = jnp.concatenate([q, q], axis=1)
        out[rows, :] = (total_rows * (1.0 / XSCALE) + PRIOR * cbuf[rows, :]) / q

    def finish_b():
        got(rbx, BX)
        rows = rows_b(0, 0)
        finish(pl.ds(RA, RB), rows, numer[rows, :] + rbx[0] + rbx[1] + rbx[2])

    def finish_a():
        got(raz.at[2], AZ + 3)
        rows = rows_a(0, 0)
        finish(pl.ds(0, RA), rows, numer[rows, :] + raz[2, 0] + raz[2, 1])

    def give(rows, kind, k, dev):
        send(out.at[rows], out.at[rows], kind, k, dev)

    def gaz_send(k):
        for e, sg in SIDES:
            if k < 3:
                give(rows_a(0, -k * sg), S_GAZ, GAZ + k, at_z(sg))
            else:
                give(rows_a(0, -3 * sg, e * HA, HA), S_GAZ, GAZ + k, at_z(sg))

    def gaz_got(k):
        got(numer.at[pl.ds(0, 2 * RA if k < 3 else RA)], GAZ + k)

    def ga1_send(i):
        for _, sg in SIDES:
            give(rows_a(0, ORDER_AG[i]), S_GA1, GA1 + i, at_x(sg))

    def ga2_send(i):
        give(rows_a(0, ORDER_AG[i]), S_GA2, GA2 + i, at_x(2))

    def ga2_step(i):
        got(numer.at[pl.ds(0, 2 * RA)], GA1 + i)
        for e, sg in SIDES:
            give(rows_a(-sg, ORDER_AG[i], e * HA, HA), S_GA2, GA2 + i, at_x(sg))

    def ga2_got(i):
        got(numer.at[pl.ds(0, RA)], GA2 + i)

    def ga2_last():
        got(numer.at[pl.ds(0, 2 * RA)], GA1 + 7)
        ga2_got(7)

    def gbx_send():
        for d in (2, 1, 3):
            give(rows_b(0, 0), S_GBX, GBX, at_x(d))

    def gbz_send(k, j):
        t = ORDER_T[j]
        for e, sg in SIDES:
            if k < 3:
                give(rows_b(-k * sg, t), S_GBZ, GBZ + 4 * j + k, at_z(sg))
            else:
                give(rows_b(-3 * sg, t, e * HB, HB), S_GBZ, GBZ + 4 * j + k, at_z(sg))

    def gbz_first():
        got(numer.at[pl.ds(0, 3 * RB)], GBX)
        for j in (1, 2, 3):
            gbz_send(0, j)

    def gbz_got(k, j):
        got(numer.at[pl.ds(0, 2 * RB if k < 3 else RB)], GBZ + 4 * j + k)

    def gbz_step(k, j):
        gbz_got(k, j)
        gbz_send(k + 1, j)

    def blocks(j, _):
        late = j // 6
        r = lax.rem(j, 3)
        dx = (2 - r - r // 2) * (1 - late)
        h = (j // 3) * (1 - late) + (j - 6) * late
        pieces = [rows_a(dx, 4 - 6 * h), rows_a(dx, 3 - 2 * h), rows_a(dx, 2 * h - 3), rows_a(dx, 2 - 2 * h)]
        block_b(pieces, f_buf[mod(x + dx, NX)])

        @pl.when(j == 0)
        def _():
            a1_send(0)

        @pl.when(j == 1)
        def _():
            bz_send0(1)
            a1_send(2)
            a1_send(1)
            bz_send0(0)
            a1_send(3)

        @pl.when(j == 3)
        def _():
            a1_step(0)

        @pl.when(j == 4)
        def _():
            bz_step(1, 1)

        @pl.when(j == 5)
        def _():
            a1_send(4)
            a1_send(6)

        @pl.when(j == 6)
        def _():
            a1_send(5)
            a2_step(0)
            az_send0()
            a1_step(3)
            a1_send(7)
            bz_step(1, 0)

        @pl.when(j == 7)
        def _():
            a2_step(1)
            bz_step(2, 1)

        dz = 4 + (1 - 2 * lax.rem(j, 2)) * ((j + 1) // 2)
        block_b([chunk_rows_b(dz)], f_buf[NX + mod(z + dz, NZ) // (NZ // NTB)])

        @pl.when(j == 4)
        def _():
            a1_step(1)
            a1_step(2)

        return 0

    lax.fori_loop(0, 8, blocks, 0)

    weights(0)
    a2_step(2)
    az_step(1)
    weights(1)
    a1_step(4)
    weights(2)
    bz_step(2, 0)
    a1_step(5)
    a1_step(6)
    weights(3)
    weights_x()
    bz_step(3, 1)
    a2_step(3)
    a1_step(7)
    a2_step(4)
    az_step(2)
    bz_step(3, 0)
    a2_step(5)
    bz_last(1)
    a2_step(6)
    weights_z()
    az_step(3)
    a2_step(7)
    bz_last(0)
    bx_send()
    weights_own()
    finish_a()
    gaz_send(0)
    ga1_send(0)
    finish_b()
    gbx_send()
    gbz_send(0, 0)
    gaz_got(0)
    gaz_send(1)
    ga1_send(1)
    ga1_send(2)
    ga2_step(0)
    gbz_step(0, 0)
    gbz_first()
    gaz_got(1)
    gaz_send(2)
    ga1_send(3)
    ga2_step(1)
    ga1_send(4)
    gbz_step(1, 0)
    ga2_step(2)
    gbz_step(0, 1)
    ga2_got(0)
    gbz_step(0, 3)
    gbz_step(0, 2)
    ga2_step(3)
    ga2_got(1)
    gaz_got(2)
    gaz_send(3)
    ga1_send(6)
    ga1_send(5)
    ga2_step(4)
    gbz_step(2, 0)
    ga2_got(2)
    gbz_step(1, 1)
    ga2_got(3)
    gbz_step(1, 3)
    gbz_step(1, 2)
    ga2_step(6)
    gaz_got(3)
    ga1_send(7)
    ga2_send(7)
    gbz_got(3, 0)
    ga2_step(5)
    gbz_step(2, 1)
    ga2_got(4)
    gbz_step(2, 3)
    ga2_got(6)
    gbz_step(2, 2)
    gbz_got(3, 1)
    gbz_got(3, 3)
    ga2_last()
    gbz_got(3, 2)
    ga2_got(5)
    sent(stat.at[pl.ds(0, NC - 1)], S_STAT)
    sent(rw1, S_W1)
    sent(rw2, S_W2)
    sent(rbx, S_BX)
    sent(rbx, S_GBX)
    sent(ra1, S_A1)
    sent(ra2, S_A2)
    for kind, rows in (
        (S_AZ, 2 * (3 * RA + HA)), (S_GAZ, 2 * (3 * RA + HA)), (S_GA1, 16 * RA), (S_GA2, 8 * RA),
        (S_BZ, 2 * (3 * CB + CB // 2)), (S_GBZ, 2 * (3 * CB + CB // 2)),
    ):
        sent(numer.at[pl.ds(0, rows)], kind)


def local(vectors, centroids):
    f32, bf16 = jnp.float32, jnp.bfloat16
    V = pltpu.VMEM
    refined, lse = pl.pallas_call(
        kernel,
        out_shape=(
            V((KP, D), f32),
            V((N,), f32),
        ),
        in_specs=[pl.BlockSpec(memory_space=pl.ANY)] * 2,
        out_specs=[pl.BlockSpec(memory_space=pltpu.VMEM)] * 2,
        scratch_shapes=[
            V((N, D), f32), V((KP, D), f32),
            V((N, D), bf16), V((N, D), bf16), V((D, N), bf16), V((D, N), bf16),
            V((KP, N), f32), V((NT, 8, N), f32), V((NT, 8, N), f32), V((NT, 8, N), f32),
            V((NC, 1, N), f32), V((KP, D), f32), V((KP, 128), f32),
            V((NX, NZ, 128), f32), V((NX - 1, NZ, 128), f32),
            V((NZ, 1, 128), f32), V((NZ - 1, 1, 128), f32),
            V((8, 2, RA // 2, D), f32), V((8, 2, RA, D), f32),
            V((2, RA // 2, D), f32), V((3, 2, RA, D), f32),
            V((Q, 2, CB // Q // 2, D), f32), V((3, Q, 2, CB // Q, D), f32),
            V((NX - 1, RB, D), f32),
            V((RA + RB, RA + RB), f32),
            pltpu.SemaphoreType.DMA((NSEND,)), pltpu.SemaphoreType.DMA((NRECV,)),
            pltpu.SemaphoreType.DMA((NT + 4,)),
        ],
        compiler_params=pltpu.CompilerParams(
            collective_id=0, has_side_effects=True, vmem_limit_bytes=50 * 1024 * 1024
        ),
    )(vectors, centroids)
    return refined, lse


def solution(mesh):
    return jax.shard_map(
        local,
        mesh=mesh,
        in_specs=(P("item", None), P("cent", None)),
        out_specs=(P("cent", None), P("item")),
        check_vma=False,
    )
```

```python
import functools
import math

import jax
import jax.numpy as jnp
from jax import lax
from jax.experimental import pallas as pl
from jax.experimental.pallas import tpu as pltpu
from jax.sharding import PartitionSpec as P

MESH = pl.DeviceIdType.MESH
BOLTZMANN_SCALE = 8.0
PRIOR = 2.0
LOG2E = math.log2(math.e)
LN2 = math.log(2.0)
XSCALE = 2.0 * LOG2E / BOLTZMANN_SCALE

NX, NZ, NC = 4, 8, 8
D = 256
N = 1024
KP = 4096
RA, RB = 80, 48
CA, CB = NZ * RA, NX * RB
B0 = NX * CA
TB = 768
NTB = NZ * CB // TB
NT = NX + NTB
Q = 2

STAT, W1, W2, BX, GBX = range(5)
A1 = 5
A2 = A1 + 8
AZ = A2 + 8
BZ = AZ + 4
GAZ = BZ + 4 * Q
GA1 = GAZ + 4
GA2 = GA1 + 8
GBZ = GA2 + 8
NRECV = GBZ + 16
S_STAT, S_W1, S_W2, S_BX, S_GBX, S_A1, S_A2, S_AZ, S_BZ, S_GAZ, S_GA1, S_GA2, S_GBZ = range(13)
NSEND = 13

ORDER_RS = (4, 3, -3, 2, -2, 1, -1, 0)
ORDER_AG = (0, -1, 1, -2, 2, -3, 3, 4)
ORDER_T = (0, -1, 1, 2)


def dot(a, b):
    return jnp.dot(a, b, preferred_element_type=jnp.float32)


def split(v):
    hi = v.astype(jnp.bfloat16)
    lo = (v - hi.astype(jnp.float32)).astype(jnp.bfloat16)
    return hi, lo


def kernel(
    x_hbm, c_hbm, out, lse_out,
    xbuf, cbuf, xh, xl, xht, xlt, e_buf, m_buf, s_buf, f_buf, stat, numer, w8,
    wown, rw1, w2s, rw2, ra1, ra2, raz0, raz, rbz0, rbz, rbx, den,
    ss, rs, lsem,
):
    item = lax.axis_index("item")
    cent = lax.axis_index("cent")
    x, z = item // NZ, lax.rem(item, NZ)

    def mod(v, n):
        return lax.rem(v + 2 * n, n)

    def at_x(d):
        return {"item": mod(x + d, NX) * NZ + z}

    def at_z(d):
        return {"item": x * NZ + mod(z + d, NZ)}

    def at_c(d):
        return {"cent": mod(cent + d, NC)}

    def copy(src, dst, kind, k, dev):
        return pltpu.make_async_remote_copy(
            src_ref=src, dst_ref=dst, send_sem=ss.at[kind], recv_sem=rs.at[k],
            device_id=dev, device_id_type=MESH,
        )

    def send(src, dst, kind, k, dev):
        copy(src, dst, kind, k, dev).start()

    def got(region, k):
        copy(region, region, 0, k, at_x(1)).wait_recv()

    def sent(region, kind):
        copy(region, region, kind, 0, at_x(1)).wait_send()

    def x_load(j):
        rows = pl.ds(j * 256, 256)
        return pltpu.make_async_copy(x_hbm.at[rows], xbuf.at[rows], lsem.at[NT + j])

    for j in range(N // 256):
        x_load(j).start()

    def tile_rows(t, rows_n, base):
        return pl.ds(pl.multiple_of(base + t * rows_n, 8), rows_n)

    def c_load(t, rows_n, base, k):
        rows = tile_rows(t, rows_n, base)
        return pltpu.make_async_copy(c_hbm.at[rows], cbuf.at[rows], lsem.at[k])

    for t in range(NX):
        c_load(t, CA, 0, t).start()
    for t in range(NTB):
        c_load(t, TB, B0, NX + t).start()

    barrier = pltpu.get_barrier_semaphore()
    for d in range(1, NX):
        pl.semaphore_signal(barrier, inc=1, device_id=at_x(d), device_id_type=MESH)
    for d in range(1, NZ):
        pl.semaphore_signal(barrier, inc=1, device_id=at_z(d), device_id_type=MESH)
    for d in range(1, NC):
        pl.semaphore_signal(barrier, inc=1, device_id=at_c(d), device_id_type=MESH)

    for j in range(N // 256):
        x_load(j).wait()
        rows = pl.ds(j * 256, 256)
        v = xbuf[rows, :] * XSCALE
        hi, lo = split(v)
        xh[rows, :] = hi
        xl[rows, :] = lo
        hi, lo = split(v.T)
        xht[:, rows] = hi
        xlt[:, rows] = lo

    def stage_a(rows_n, base, first):
        def tile(t, _):
            c_load(t, rows_n, base, first + t).wait()
            rows = tile_rows(t, rows_n, base)
            c = cbuf[rows, :]
            csq = jnp.sum(c * c, axis=1, keepdims=True) * (LOG2E / BOLTZMANN_SCALE)
            ch, cl = split(c)
            for j in range(N // 256):
                cols = pl.ds(j * 256, 256)
                b = xht[:, cols]
                l = dot(ch, b) + dot(cl, b) + dot(ch, xlt[:, cols]) - csq
                l = l.reshape(rows_n // 8, 8, 256)
                m = jnp.max(l, axis=0)
                e = jnp.exp2(l - m[None])
                e_buf[rows, cols] = e.reshape(rows_n, 256)
                m_buf[first + t, :, cols] = m
                s_buf[first + t, :, cols] = jnp.sum(e, axis=0)
            return 0

        return tile

    lax.fori_loop(0, NX, stage_a(CA, 0, 0), 0)
    lax.fori_loop(0, NTB, stage_a(TB, B0, NX), 0)

    mm = m_buf[...]
    m_loc = jnp.max(jnp.max(mm, axis=0), axis=0, keepdims=True)
    s_loc = jnp.sum(
        jnp.sum(s_buf[...] * jnp.exp2(mm - m_loc[None]), axis=0), axis=0, keepdims=True
    )
    stat[cent] = m_loc + jnp.log(s_loc) * LOG2E
    pl.semaphore_wait(barrier, (NX - 1) + (NZ - 1) + (NC - 1))
    for d in range(1, NC):
        send(stat.at[cent], stat.at[cent], S_STAT, STAT, at_c(d))
    got(stat.at[pl.ds(0, NC - 1)], STAT)
    parts = stat[...]
    top = jnp.max(parts, axis=0)
    total = jnp.log(jnp.sum(jnp.exp2(parts - top[None]), axis=0))
    lse_out[...] = (top * LN2 + total).reshape(N)
    lse2 = top + total * LOG2E
    f_buf[...] = jnp.exp2(mm - lse2[None])

    def block_b(pieces, f):
        hs, ls = [], []
        for rows in pieces:
            n = rows.size
            p = (e_buf[rows, :].reshape(n // 8, 8, N) * f[None]).reshape(n, N)
            w = p[:, 0:128]
            for q in range(1, N // 128):
                w = w + p[:, q * 128 : (q + 1) * 128]
            w8[rows, :] = w
            hi, lo = split(p)
            hs.append(hi)
            ls.append(lo)
        hi = jnp.concatenate(hs, axis=0)
        lo = jnp.concatenate(ls, axis=0)
        r = dot(hi, xh[...]) + dot(lo, xh[...]) + dot(hi, xl[...])
        at = 0
        for rows in pieces:
            numer[rows, :] = r[at : at + rows.size]
            at += rows.size

    def rows_a(dx, dz, off=0, n=RA):
        return pl.ds(pl.multiple_of(mod(x + dx, NX) * CA + mod(z + dz, NZ) * RA + off, 8), n)

    def rows_b(dz, dx, off=0, n=RB):
        return pl.ds(pl.multiple_of(B0 + mod(z + dz, NZ) * CB + mod(x + dx, NX) * RB + off, 8), n)

    def chunk_rows_b(dz, off=0, n=CB):
        return pl.ds(pl.multiple_of(B0 + mod(z + dz, NZ) * CB + off, 8), n)

    def add(rows, ref):
        numer[rows, :] += ref[...]

    HA, HB = RA // 2, RB // 2
    CQ = CB // Q
    HQ = CQ // 2

    SIDES = ((0, 1), (1, -1))

    def a1_send(i):
        for e, sg in SIDES:
            send(numer.at[rows_a(2, ORDER_RS[i], e * HA, HA)], ra1.at[i, e], S_A1, A1 + i, at_x(sg))

    def a1_step(i):
        o = ORDER_RS[i]
        got(ra1.at[i], A1 + i)
        for e, sg in SIDES:
            add(rows_a(sg, o, e * HA, HA), ra1.at[i, e])
            send(numer.at[rows_a(sg, o)], ra2.at[i, e], S_A2, A2 + i, at_x(sg))

    def a2_step(i):
        got(ra2.at[i], A2 + i)
        numer[rows_a(0, ORDER_RS[i]), :] += ra2[i, 0] + ra2[i, 1]

    def az_send0():
        for e, sg in SIDES:
            send(numer.at[rows_a(0, 4, e * HA, HA)], raz0.at[e], S_AZ, AZ, at_z(sg))

    def az_step(k):
        got(raz0 if k == 1 else raz.at[k - 2], AZ + k - 1)
        for e, sg in SIDES:
            if k == 1:
                add(rows_a(0, 3 * sg, e * HA, HA), raz0.at[e])
            else:
                add(rows_a(0, (4 - k) * sg), raz.at[k - 2, e])
            send(numer.at[rows_a(0, (4 - k) * sg)], raz.at[k - 1, e], S_AZ, AZ + k, at_z(sg))

    def bz_send0(q):
        for e, sg in SIDES:
            send(
                numer.at[chunk_rows_b(4, q * CQ + e * HQ, HQ)], rbz0.at[q, e],
                S_BZ, BZ + 4 * q, at_z(sg))

    def bz_step(k, q):
        got(rbz0.at[q] if k == 1 else rbz.at[k - 2, q], BZ + 4 * q + k - 1)
        for e, sg in SIDES:
            if k == 1:
                add(chunk_rows_b(3 * sg, q * CQ + e * HQ, HQ), rbz0.at[q, e])
            else:
                add(chunk_rows_b((4 - k) * sg, q * CQ, CQ), rbz.at[k - 2, q, e])
            send(
                numer.at[chunk_rows_b((4 - k) * sg, q * CQ, CQ)], rbz.at[k - 1, q, e],
                S_BZ, BZ + 4 * q + k, at_z(sg))

    def bz_last(q):
        got(rbz.at[2, q], BZ + 4 * q + 3)
        numer[chunk_rows_b(0, q * CQ, CQ), :] += rbz[2, q, 0] + rbz[2, q, 1]

    def owner_weights(xd, zd):
        a = w8[pl.ds(xd * CA + zd * RA, RA), :]
        b = w8[pl.ds(B0 + zd * CB + xd * RB, RB), :]
        t = jnp.concatenate([a, b], axis=0).T
        wown[xd, zd : zd + 1, :] = jnp.sum(t, axis=0, keepdims=True)

    def weights(k):
        for i in range(8 * k, 8 * k + 8):
            owner_weights(*divmod(i, NZ))

    def weights_x():
        for d in range(1, NX):
            send(wown.at[mod(x + d, NX)], rw1.at[d - 1], S_W1, W1, at_x(d))

    def weights_z():
        got(rw1, W1)
        w = wown[x] + rw1[0] + rw1[1] + rw1[2]
        for s in range(NZ):
            w2s[s] = w[s : s + 1, :]
        for d in range(1, NZ):
            send(w2s.at[mod(z + d, NZ)], rw2.at[d - 1], S_W2, W2, at_z(d))

    def weights_own():
        got(rw2, W2)
        w = w2s[z]
        for d in range(1, NZ):
            w = w + rw2[d - 1]
        den[...] = jnp.broadcast_to(w, (RA + RB, RA + RB)).T + PRIOR

    def bx_send():
        for d in range(1, NX):
            send(numer.at[rows_b(0, d)], rbx.at[d - 1], S_BX, BX, at_x(d))

    def finish(mine, rows, total_rows):
        q = den[mine, :]
        q = jnp.concatenate([q, q], axis=1)
        out[rows, :] = (total_rows * (1.0 / XSCALE) + PRIOR * cbuf[rows, :]) / q

    def finish_b():
        got(rbx, BX)
        rows = rows_b(0, 0)
        finish(pl.ds(RA, RB), rows, numer[rows, :] + rbx[0] + rbx[1] + rbx[2])

    def finish_a():
        got(raz.at[2], AZ + 3)
        rows = rows_a(0, 0)
        finish(pl.ds(0, RA), rows, numer[rows, :] + raz[2, 0] + raz[2, 1])

    def give(rows, kind, k, dev):
        send(out.at[rows], out.at[rows], kind, k, dev)

    def gaz_send(k):
        for e, sg in SIDES:
            if k < 3:
                give(rows_a(0, -k * sg), S_GAZ, GAZ + k, at_z(sg))
            else:
                give(rows_a(0, -3 * sg, e * HA, HA), S_GAZ, GAZ + k, at_z(sg))

    def gaz_got(k):
        got(numer.at[pl.ds(0, 2 * RA if k < 3 else RA)], GAZ + k)

    def ga1_send(i):
        for _, sg in SIDES:
            give(rows_a(0, ORDER_AG[i]), S_GA1, GA1 + i, at_x(sg))

    def ga2_send(i):
        give(rows_a(0, ORDER_AG[i]), S_GA2, GA2 + i, at_x(2))

    def ga2_step(i):
        got(numer.at[pl.ds(0, 2 * RA)], GA1 + i)
        for e, sg in SIDES:
            give(rows_a(-sg, ORDER_AG[i], e * HA, HA), S_GA2, GA2 + i, at_x(sg))

    def ga2_got(i):
        got(numer.at[pl.ds(0, RA)], GA2 + i)

    def ga2_last():
        got(numer.at[pl.ds(0, 2 * RA)], GA1 + 7)
        ga2_got(7)

    def gbx_send():
        for d in (2, 1, 3):
            give(rows_b(0, 0), S_GBX, GBX, at_x(d))

    def gbz_send(k, j):
        t = ORDER_T[j]
        for e, sg in SIDES:
            if k < 3:
                give(rows_b(-k * sg, t), S_GBZ, GBZ + 4 * j + k, at_z(sg))
            else:
                give(rows_b(-3 * sg, t, e * HB, HB), S_GBZ, GBZ + 4 * j + k, at_z(sg))

    def gbz_first():
        got(numer.at[pl.ds(0, 3 * RB)], GBX)
        for j in (1, 2, 3):
            gbz_send(0, j)

    def gbz_got(k, j):
        got(numer.at[pl.ds(0, 2 * RB if k < 3 else RB)], GBZ + 4 * j + k)

    def gbz_step(k, j):
        gbz_got(k, j)
        gbz_send(k + 1, j)

    def part_a(dx, half):
        order = ORDER_RS[4 * half : 4 * half + 4]
        block_b([rows_a(dx, o) for o in order], f_buf[mod(x + dx, NX)])

    def part_b(dz):
        block_b([chunk_rows_b(dz)], f_buf[NX + mod(z + dz, NZ) // (NZ // NTB)])

    part_a(2, 0)
    a1_send(0)
    part_b(4)
    bz_send0(1)
    a1_send(2)
    a1_send(1)
    part_a(2, 1)
    a1_send(4)
    part_a(1, 0)
    part_a(0, 0)
    part_a(-1, 0)
    part_b(-2)
    a1_step(0)
    part_b(1)
    part_b(-3)
    a1_step(2)
    bz_send0(0)
    part_b(3)
    bz_step(1, 1)
    a1_step(1)
    part_a(1, 1)
    part_b(-1)
    a1_send(3)
    part_a(-1, 1)
    a1_step(4)
    a1_send(5)
    part_a(0, 1)
    a2_step(0)
    az_send0()
    part_b(0)
    bz_step(1, 0)
    a1_send(6)
    part_b(2)
    a1_send(7)
    weights(0)
    weights(1)
    bz_step(2, 1)
    weights(2)
    a2_step(2)
    weights(3)
    weights_x()
    a2_step(1)
    az_step(1)
    a1_step(3)
    bz_step(2, 0)
    a2_step(4)
    a1_step(5)
    a1_step(6)
    bz_step(3, 1)
    a1_step(7)
    weights_z()
    a2_step(3)
    az_step(2)
    bz_step(3, 0)
    a2_step(5)
    bz_last(1)
    weights_own()
    a2_step(6)
    az_step(3)
    a2_step(7)
    bz_last(0)
    bx_send()
    finish_a()
    gaz_send(0)
    ga1_send(0)
    finish_b()
    gbx_send()
    gbz_send(0, 0)
    gaz_got(0)
    gaz_send(1)
    ga2_step(0)
    ga1_send(2)
    ga1_send(1)
    gbz_step(0, 0)
    gbz_first()
    ga2_got(0)
    gaz_got(1)
    gaz_send(2)
    ga1_send(4)
    ga1_send(3)
    ga2_step(2)
    gbz_step(1, 0)
    gbz_step(0, 2)
    ga2_step(1)
    gbz_step(0, 1)
    gbz_step(0, 3)
    ga2_step(4)
    gaz_got(2)
    gaz_send(3)
    ga1_send(5)
    ga1_send(6)
    ga2_step(3)
    ga2_got(2)
    gbz_step(2, 0)
    ga2_got(1)
    gbz_step(1, 2)
    ga2_got(4)
    gbz_step(1, 1)
    gbz_step(1, 3)
    ga2_step(5)
    gaz_got(3)
    ga1_send(7)
    ga2_send(7)
    gbz_got(3, 0)
    ga2_step(6)
    gbz_step(2, 2)
    ga2_got(3)
    gbz_step(2, 1)
    ga2_got(5)
    gbz_step(2, 3)
    gbz_got(3, 2)
    gbz_got(3, 1)
    ga2_last()
    gbz_got(3, 3)
    ga2_got(6)

    sent(stat.at[pl.ds(0, NC - 1)], S_STAT)
    sent(rw1, S_W1)
    sent(rw2, S_W2)
    sent(rbx, S_BX)
    sent(rbx, S_GBX)
    sent(ra1, S_A1)
    sent(ra2, S_A2)
    for kind, rows in (
        (S_AZ, 2 * (3 * RA + HA)), (S_GAZ, 2 * (3 * RA + HA)), (S_GA1, 16 * RA), (S_GA2, 8 * RA),
        (S_BZ, 2 * (3 * CB + CB // 2)), (S_GBZ, 2 * (3 * CB + CB // 2)),
    ):
        sent(numer.at[pl.ds(0, rows)], kind)


def local(vectors, centroids):
    f32, bf16 = jnp.float32, jnp.bfloat16
    V = pltpu.VMEM
    refined, lse = pl.pallas_call(
        kernel,
        out_shape=(
            V((KP, D), f32),
            V((N,), f32),
        ),
        in_specs=[pl.BlockSpec(memory_space=pl.ANY)] * 2,
        out_specs=[pl.BlockSpec(memory_space=pltpu.VMEM)] * 2,
        scratch_shapes=[
            V((N, D), f32), V((KP, D), f32),
            V((N, D), bf16), V((N, D), bf16), V((D, N), bf16), V((D, N), bf16),
            V((KP, N), f32), V((NT, 8, N), f32), V((NT, 8, N), f32), V((NT, 8, N), f32),
            V((NC, 1, N), f32), V((KP, D), f32), V((KP, 128), f32),
            V((NX, NZ, 128), f32), V((NX - 1, NZ, 128), f32),
            V((NZ, 1, 128), f32), V((NZ - 1, 1, 128), f32),
            V((8, 2, RA // 2, D), f32), V((8, 2, RA, D), f32),
            V((2, RA // 2, D), f32), V((3, 2, RA, D), f32),
            V((Q, 2, CB // Q // 2, D), f32), V((3, Q, 2, CB // Q, D), f32),
            V((NX - 1, RB, D), f32),
            V((RA + RB, RA + RB), f32),
            pltpu.SemaphoreType.DMA((NSEND,)), pltpu.SemaphoreType.DMA((NRECV,)),
            pltpu.SemaphoreType.DMA((NT + 4,)),
        ],
        compiler_params=pltpu.CompilerParams(
            collective_id=0, has_side_effects=True, vmem_limit_bytes=50 * 1024 * 1024
        ),
    )(vectors, centroids)
    return refined, lse


def solution(mesh):
    return jax.shard_map(
        local,
        mesh=mesh,
        in_specs=(P("item", None), P("cent", None)),
        out_specs=(P("cent", None), P("item")),
        check_vma=False,
    )
```

```python
import functools
import math

import jax
import jax.numpy as jnp
from jax import lax
from jax.experimental import pallas as pl
from jax.experimental.pallas import tpu as pltpu
from jax.sharding import PartitionSpec as P

MESH = pl.DeviceIdType.MESH
BOLTZMANN_SCALE = 8.0
PRIOR = 2.0
LOG2E = math.log2(math.e)
LN2 = math.log(2.0)
XSCALE = 2.0 * LOG2E / BOLTZMANN_SCALE

NX, NZ, NC = 4, 8, 8
D = 256
N = 1024
KP = 4096
RA, RB = 80, 48
CA, CB = NZ * RA, NX * RB
B0 = NX * CA
TB = 768
NTB = NZ * CB // TB
NT = NX + NTB
Q = 2
PA, PB = RA // Q, RB // Q
CQ = NX * PB
HALF_A = (((0, 24), (24, 16)), ((0, 16), (16, 24)))
HALF_B = (((0, 16), (16, 8)), ((0, 8), (8, 16)))

STAT, W1, W2 = range(3)
BX = 3
GBX = BX + Q
A1 = GBX + Q
A2 = A1 + 8 * Q
AZ = A2 + 8 * Q
BZ = AZ + 4 * Q
GAZ = BZ + 4 * Q
GA1 = GAZ + 4 * Q
GA2 = GA1 + 8 * Q
GBZ = GA2 + Q
GBL = GBZ + 12 * Q
NRECV = GBL + Q
S_STAT, S_W1, S_W2, S_BX, S_GBX, S_A1, S_A2, S_AZ, S_BZ, S_GAZ, S_GA1, S_GA2, S_GBZ = range(13)
NSEND = 13

ORDER_RS = (4, 3, -3, 2, -2, 1, -1, 0)
ORDER_AG = (0, -1, 1, -2, 2, -3, 3, 4)
ORDER_T = (0, -1, 1, 2)


def dot(a, b):
    return jnp.dot(a, b, preferred_element_type=jnp.float32)


def split(v):
    hi = v.astype(jnp.bfloat16)
    lo = (v - hi.astype(jnp.float32)).astype(jnp.bfloat16)
    return hi, lo


def kernel(
    x_hbm, c_hbm, out, lse_out,
    xbuf, cbuf, xh, xl, xht, xlt, e_buf, m_buf, s_buf, f_buf, stat, numer, w8,
    wown, rw1, w2s, rw2, ra1, ra2, raz0, raz, rbz0, rbz, rbx, den,
    ss, rs, lsem,
):
    item = lax.axis_index("item")
    cent = lax.axis_index("cent")
    x, z = item // NZ, lax.rem(item, NZ)

    def mod(v, n):
        return lax.rem(v + 2 * n, n)

    def at_x(d):
        return {"item": mod(x + d, NX) * NZ + z}

    def at_z(d):
        return {"item": x * NZ + mod(z + d, NZ)}

    def at_c(d):
        return {"cent": mod(cent + d, NC)}

    def copy(src, dst, kind, k, dev):
        return pltpu.make_async_remote_copy(
            src_ref=src, dst_ref=dst, send_sem=ss.at[kind], recv_sem=rs.at[k],
            device_id=dev, device_id_type=MESH,
        )

    def send(src, dst, kind, k, dev):
        copy(src, dst, kind, k, dev).start()

    def got(region, k):
        copy(region, region, 0, k, at_x(1)).wait_recv()

    def sent(region, kind):
        copy(region, region, kind, 0, at_x(1)).wait_send()

    def x_load(j):
        rows = pl.ds(j * 256, 256)
        return pltpu.make_async_copy(x_hbm.at[rows], xbuf.at[rows], lsem.at[NT + j])

    for j in range(N // 256):
        x_load(j).start()

    def tile_rows(t, rows_n, base):
        return pl.ds(pl.multiple_of(base + t * rows_n, 8), rows_n)

    def c_load(t, rows_n, base, k):
        rows = tile_rows(t, rows_n, base)
        return pltpu.make_async_copy(c_hbm.at[rows], cbuf.at[rows], lsem.at[k])

    for t in range(NX):
        c_load(t, CA, 0, t).start()
    for t in range(NTB):
        c_load(t, TB, B0, NX + t).start()

    barrier = pltpu.get_barrier_semaphore()
    for d in range(1, NX):
        pl.semaphore_signal(barrier, inc=1, device_id=at_x(d), device_id_type=MESH)
    for d in range(1, NZ):
        pl.semaphore_signal(barrier, inc=1, device_id=at_z(d), device_id_type=MESH)
    for d in range(1, NC):
        pl.semaphore_signal(barrier, inc=1, device_id=at_c(d), device_id_type=MESH)

    for j in range(N // 256):
        x_load(j).wait()
        rows = pl.ds(j * 256, 256)
        v = xbuf[rows, :] * XSCALE
        hi, lo = split(v)
        xh[rows, :] = hi
        xl[rows, :] = lo
        hi, lo = split(v.T)
        xht[:, rows] = hi
        xlt[:, rows] = lo

    def stage_a(rows_n, base, first):
        def tile(t, _):
            c_load(t, rows_n, base, first + t).wait()
            rows = tile_rows(t, rows_n, base)
            c = cbuf[rows, :]
            csq = jnp.sum(c * c, axis=1, keepdims=True) * (LOG2E / BOLTZMANN_SCALE)
            ch, cl = split(c)
            for j in range(N // 256):
                cols = pl.ds(j * 256, 256)
                b = xht[:, cols]
                l = dot(ch, b) + dot(cl, b) + dot(ch, xlt[:, cols]) - csq
                l = l.reshape(rows_n // 8, 8, 256)
                m = jnp.max(l, axis=0)
                e = jnp.exp2(l - m[None])
                e_buf[rows, cols] = e.reshape(rows_n, 256)
                m_buf[first + t, :, cols] = m
                s_buf[first + t, :, cols] = jnp.sum(e, axis=0)
            return 0

        return tile

    lax.fori_loop(0, NX, stage_a(CA, 0, 0), 0)
    lax.fori_loop(0, NTB, stage_a(TB, B0, NX), 0)

    mm = m_buf[...]
    m_loc = jnp.max(jnp.max(mm, axis=0), axis=0, keepdims=True)
    s_loc = jnp.sum(
        jnp.sum(s_buf[...] * jnp.exp2(mm - m_loc[None]), axis=0), axis=0, keepdims=True
    )
    stat[cent] = m_loc + jnp.log(s_loc) * LOG2E
    pl.semaphore_wait(barrier, (NX - 1) + (NZ - 1) + (NC - 1))
    for d in range(1, NC):
        send(stat.at[cent], stat.at[cent], S_STAT, STAT, at_c(d))
    got(stat.at[pl.ds(0, NC - 1)], STAT)
    parts = stat[...]
    top = jnp.max(parts, axis=0)
    total = jnp.log(jnp.sum(jnp.exp2(parts - top[None]), axis=0))
    lse2 = top + total * LOG2E
    lse_out[...] = lse2.reshape(N)
    f_buf[...] = jnp.exp2(mm - lse2[None])

    def block_b(pieces, f):
        hs, ls = [], []
        for rows in pieces:
            n = rows.size
            p = (e_buf[rows, :].reshape(n // 8, 8, N) * f[None]).reshape(n, N)
            w = p[:, 0:128]
            for q in range(1, N // 128):
                w = w + p[:, q * 128 : (q + 1) * 128]
            w8[rows, :] = w
            hi, lo = split(p)
            hs.append(hi)
            ls.append(lo)
        hi = jnp.concatenate(hs, axis=0)
        lo = jnp.concatenate(ls, axis=0)
        r = dot(hi, xh[...]) + dot(lo, xh[...]) + dot(hi, xl[...])
        at = 0
        for rows in pieces:
            numer[rows, :] = r[at : at + rows.size]
            at += rows.size

    def rows_a(dx, dz, l, off=0, n=PA):
        start = mod(x + dx, NX) * CA + l * NZ * PA + mod(z + dz, NZ) * PA + off
        return pl.ds(pl.multiple_of(start, 8), n)

    def rows_b(dz, dx, l, off=0, n=PB):
        start = B0 + mod(z + dz, NZ) * CB + l * CQ + mod(x + dx, NX) * PB + off
        return pl.ds(pl.multiple_of(start, 8), n)

    def chunk_rows_b(dz, off=0, n=CB):
        return pl.ds(pl.multiple_of(B0 + mod(z + dz, NZ) * CB + off, 8), n)

    def add(rows, ref):
        numer[rows, :] += ref[...]

    HQ = CQ // 2
    SIDES = ((0, 1), (1, -1))

    def a1_send(l, i):
        for e, sg in SIDES:
            off, n = HALF_A[l][e]
            send(
                numer.at[rows_a(2, ORDER_RS[i], l, off, n)], ra1.at[l, i, pl.ds(off, n)],
                S_A1, A1 + 8 * l + i, at_x(sg))

    def a1_step(l, i):
        o = ORDER_RS[i]
        got(ra1.at[l, i], A1 + 8 * l + i)
        for e, sg in SIDES:
            off, n = HALF_A[l][e]
            add(rows_a(sg, o, l, off, n), ra1.at[l, i, pl.ds(off, n)])
            send(numer.at[rows_a(sg, o, l)], ra2.at[l, i, e], S_A2, A2 + 8 * l + i, at_x(sg))

    def a2_step(l, i):
        got(ra2.at[l, i], A2 + 8 * l + i)
        numer[rows_a(0, ORDER_RS[i], l), :] += ra2[l, i, 0] + ra2[l, i, 1]

    def az_send0(l):
        for e, sg in SIDES:
            off, n = HALF_A[l][e]
            send(
                numer.at[rows_a(0, 4, l, off, n)], raz0.at[l, pl.ds(off, n)],
                S_AZ, AZ + 4 * l, at_z(sg))

    def az_step(l, k):
        got(raz0.at[l] if k == 1 else raz.at[l, k - 2], AZ + 4 * l + k - 1)
        for e, sg in SIDES:
            if k == 1:
                off, n = HALF_A[l][e]
                add(rows_a(0, 3 * sg, l, off, n), raz0.at[l, pl.ds(off, n)])
            else:
                add(rows_a(0, (4 - k) * sg, l), raz.at[l, k - 2, e])
            send(
                numer.at[rows_a(0, (4 - k) * sg, l)], raz.at[l, k - 1, e],
                S_AZ, AZ + 4 * l + k, at_z(sg))

    def bz_send0(q):
        for e, sg in SIDES:
            send(
                numer.at[chunk_rows_b(4, q * CQ + e * HQ, HQ)], rbz0.at[q, e],
                S_BZ, BZ + 4 * q, at_z(sg))

    def bz_step(k, q):
        got(rbz0.at[q] if k == 1 else rbz.at[k - 2, q], BZ + 4 * q + k - 1)
        for e, sg in SIDES:
            if k == 1:
                add(chunk_rows_b(3 * sg, q * CQ + e * HQ, HQ), rbz0.at[q, e])
            else:
                add(chunk_rows_b((4 - k) * sg, q * CQ, CQ), rbz.at[k - 2, q, e])
            send(
                numer.at[chunk_rows_b((4 - k) * sg, q * CQ, CQ)], rbz.at[k - 1, q, e],
                S_BZ, BZ + 4 * q + k, at_z(sg))

    def bz_last(q):
        got(rbz.at[2, q], BZ + 4 * q + 3)
        numer[chunk_rows_b(0, q * CQ, CQ), :] += rbz[2, q, 0] + rbz[2, q, 1]

    def owner_weights(xd, zd):
        a, b = xd * CA + zd * PA, B0 + zd * CB + xd * PB
        rows = [pl.ds(a + l * NZ * PA, PA) for l in range(Q)] + [pl.ds(b + l * CQ, PB) for l in range(Q)]
        t = jnp.concatenate([w8[r, :] for r in rows], axis=0).T
        wown[xd, zd : zd + 1, :] = jnp.sum(t, axis=0, keepdims=True)

    def weights(k):
        for i in range(8 * k, 8 * k + 8):
            owner_weights(*divmod(i, NZ))

    def weights_x():
        for d in range(1, NX):
            send(wown.at[mod(x + d, NX)], rw1.at[d - 1], S_W1, W1, at_x(d))

    def weights_z():
        got(rw1, W1)
        w = wown[x] + rw1[0] + rw1[1] + rw1[2]
        for s in range(NZ):
            w2s[s] = w[s : s + 1, :]
        for d in range(1, NZ):
            send(w2s.at[mod(z + d, NZ)], rw2.at[d - 1], S_W2, W2, at_z(d))

    def weights_own():
        got(rw2, W2)
        w = w2s[z]
        for d in range(1, NZ):
            w = w + rw2[d - 1]
        den[...] = jnp.broadcast_to(w, (RA + RB, RA + RB)).T + PRIOR

    def bx_send(l):
        for d in range(1, NX):
            send(numer.at[rows_b(0, d, l)], rbx.at[l, d - 1], S_BX, BX + l, at_x(d))

    def finish(mine, rows, total_rows):
        q = den[mine, :]
        q = jnp.concatenate([q, q], axis=1)
        out[rows, :] = (total_rows * (1.0 / XSCALE) + PRIOR * cbuf[rows, :]) / q

    def finish_b(l):
        got(rbx.at[l], BX + l)
        rows = rows_b(0, 0, l)
        finish(pl.ds(RA + l * PB, PB), rows, numer[rows, :] + rbx[l, 0] + rbx[l, 1] + rbx[l, 2])

    def finish_a(l):
        got(raz.at[l, 2], AZ + 4 * l + 3)
        rows = rows_a(0, 0, l)
        finish(pl.ds(l * PA, PA), rows, numer[rows, :] + raz[l, 2, 0] + raz[l, 2, 1])

    def give(rows, kind, k, dev):
        send(out.at[rows], out.at[rows], kind, k, dev)

    def gaz_send(l, k):
        for e, sg in SIDES:
            rows = rows_a(0, -k * sg, l) if k < 3 else rows_a(0, -3 * sg, l, *HALF_A[l][e])
            give(rows, S_GAZ, GAZ + 4 * l + k, at_z(sg))

    def gaz_got(l, k):
        got(numer.at[pl.ds(0, 2 * PA if k < 3 else PA)], GAZ + 4 * l + k)

    def ga1_send(l, i):
        for _, sg in SIDES:
            give(rows_a(0, ORDER_AG[i], l), S_GA1, GA1 + 8 * l + i, at_x(sg))

    def ga1_got(l, i):
        got(numer.at[pl.ds(0, 2 * PA)], GA1 + 8 * l + i)

    def ga2_send(l, i):
        give(rows_a(0, ORDER_AG[i], l), S_GA2, GA2 + l, at_x(2))

    def ga2_step(l, i):
        ga1_got(l, i)
        for e, sg in SIDES:
            give(rows_a(-sg, ORDER_AG[i], l, *HALF_A[l][e]), S_GA2, GA2 + l, at_x(sg))

    def gbx_send(l):
        for d in (2, 1, 3):
            give(rows_b(0, 0, l), S_GBX, GBX + l, at_x(d))

    def gbz_send(l, k, j):
        t = ORDER_T[j]
        for e, sg in SIDES:
            if k < 3:
                give(rows_b(-k * sg, t, l), S_GBZ, GBZ + 12 * l + 3 * j + k, at_z(sg))
            else:
                give(rows_b(-3 * sg, t, l, *HALF_B[l][e]), S_GBZ, GBL + l, at_z(sg))

    def gbz_first(l):
        got(numer.at[pl.ds(0, 3 * PB)], GBX + l)
        for j in (1, 2, 3):
            gbz_send(l, 0, j)

    def gbz_step(l, k, j):
        got(numer.at[pl.ds(0, 2 * PB)], GBZ + 12 * l + 3 * j + k)
        gbz_send(l, k + 1, j)

    def part_a(dx, l):
        start = mod(x + dx, NX) * CA + l * NZ * PA
        block_b([pl.ds(pl.multiple_of(start, 8), NZ * PA)], f_buf[mod(x + dx, NX)])

    def part_b(dz):
        block_b([chunk_rows_b(dz)], f_buf[NX + mod(z + dz, NZ) // (NZ // NTB)])

    part_b(4)
    bz_send0(0)
    bz_send0(1)
    part_a(2, 0)
    a1_send(0, 0)
    a1_send(0, 1)
    part_a(2, 1)
    a1_send(1, 3)
    a1_send(1, 0)
    a1_send(1, 1)
    part_b(3)
    part_b(-3)
    part_a(1, 0)
    part_a(-1, 0)
    a1_send(0, 2)
    a1_send(1, 2)
    bz_step(1, 0)
    a1_step(0, 0)
    a1_send(0, 4)
    a1_send(1, 4)
    part_a(1, 1)
    bz_step(1, 1)
    a1_send(0, 3)
    part_a(-1, 1)
    a1_step(1, 0)
    a1_step(1, 1)
    part_a(0, 1)
    a1_step(0, 1)
    a1_step(0, 2)
    part_b(-2)
    a1_step(1, 2)
    part_a(0, 0)
    a1_send(0, 5)
    a2_step(0, 0)
    az_send0(0)
    a1_send(0, 6)
    part_b(2)
    bz_step(2, 0)
    a1_step(0, 4)
    a1_step(1, 4)
    a1_send(1, 5)
    a1_send(1, 6)
    a1_step(0, 3)
    a1_send(1, 7)
    a1_send(0, 7)
    a1_step(1, 3)
    part_b(-1)
    a2_step(1, 0)
    az_send0(1)
    part_b(1)
    bz_step(2, 1)
    part_b(0)
    a2_step(1, 1)
    weights(0)
    weights(1)
    weights(2)
    weights(3)
    a2_step(0, 1)
    weights_x()
    a2_step(0, 2)
    az_step(0, 1)
    bz_step(3, 0)
    a2_step(1, 2)
    az_step(1, 1)
    a1_step(0, 5)
    a1_step(0, 6)
    a2_step(0, 4)
    bz_step(3, 1)
    a2_step(1, 4)
    a1_step(1, 5)
    a1_step(1, 6)
    a2_step(0, 3)
    az_step(0, 2)
    a1_step(1, 7)
    a1_step(0, 7)
    bz_last(0)
    bx_send(0)
    a2_step(1, 3)
    az_step(1, 2)
    weights_z()
    a2_step(0, 5)
    a2_step(0, 6)
    bz_last(1)
    bx_send(1)
    a2_step(1, 5)
    az_step(0, 3)
    a2_step(1, 6)
    az_step(1, 3)
    weights_own()
    a2_step(1, 7)
    a2_step(0, 7)
    finish_b(0)
    gbz_send(0, 0, 0)
    finish_a(0)
    gaz_send(0, 0)
    gbx_send(0)
    ga1_send(0, 0)
    finish_b(1)
    gbx_send(1)
    finish_a(1)
    ga1_send(1, 0)
    gaz_send(1, 0)
    gbz_send(1, 0, 0)
    gbz_step(0, 0, 0)
    gaz_got(0, 0)
    gaz_send(0, 1)
    ga1_send(0, 1)
    gbz_first(0)
    ga1_send(0, 2)
    gaz_got(1, 0)
    gaz_send(1, 1)
    ga1_send(1, 2)
    ga1_send(1, 1)
    ga2_step(0, 0)
    gbz_step(1, 0, 0)
    gbz_first(1)
    gbz_step(0, 1, 0)
    ga2_step(1, 0)
    gaz_got(0, 1)
    gaz_send(0, 2)
    ga1_send(0, 3)
    ga2_step(0, 1)
    ga1_send(0, 4)
    gbz_step(0, 0, 3)
    ga2_step(0, 2)
    gbz_step(0, 0, 2)
    gbz_step(0, 0, 1)
    ga2_step(1, 2)
    gaz_got(1, 1)
    gaz_send(1, 2)
    ga1_send(1, 4)
    ga2_step(1, 1)
    ga1_send(1, 3)
    gbz_step(1, 1, 0)
    gbz_step(1, 0, 3)
    gbz_step(1, 0, 2)
    ga2_step(0, 3)
    gbz_step(1, 0, 1)
    gbz_step(0, 2, 0)
    ga2_step(0, 4)
    gaz_got(0, 2)
    gaz_send(0, 3)
    ga1_send(0, 6)
    ga1_send(0, 5)
    gbz_step(0, 1, 3)
    gbz_step(0, 1, 2)
    gbz_step(0, 1, 1)
    ga2_step(1, 4)
    gaz_got(1, 2)
    gaz_send(1, 3)
    ga1_send(1, 6)
    ga1_send(1, 5)
    ga2_step(1, 3)
    gbz_step(1, 2, 0)
    gbz_step(1, 1, 3)
    gbz_step(1, 1, 2)
    gbz_step(1, 1, 1)
    ga2_step(0, 6)
    gaz_got(0, 3)
    ga1_send(0, 7)
    ga2_step(0, 5)
    gbz_step(0, 2, 3)
    gbz_step(0, 2, 2)
    gbz_step(0, 2, 1)
    ga2_step(1, 6)
    gaz_got(1, 3)
    ga1_send(1, 7)
    ga2_send(1, 7)
    ga2_step(1, 5)
    gbz_step(1, 2, 3)
    gbz_step(1, 2, 2)
    gbz_step(1, 2, 1)
    ga2_step(0, 7)
    for l in range(Q):
        got(numer.at[pl.ds(0, NX * PB)], GBL + l)
        got(numer.at[pl.ds(0, 8 * PA)], GA2 + l)
    ga1_got(1, 7)

    sent(stat.at[pl.ds(0, NC - 1)], S_STAT)
    sent(rw1, S_W1)
    sent(rw2, S_W2)
    sent(rbx, S_BX)
    sent(rbx, S_GBX)
    sent(ra1, S_A1)
    sent(ra2, S_A2)
    for kind, rows in (
        (S_AZ, 7 * RA), (S_GAZ, 7 * RA), (S_GA1, 16 * RA), (S_GA2, 8 * RA),
        (S_BZ, 7 * CB), (S_GBZ, 7 * CB),
    ):
        sent(numer.at[pl.ds(0, rows)], kind)


def local(vectors, centroids):
    f32, bf16 = jnp.float32, jnp.bfloat16
    V = pltpu.VMEM
    refined, lse = pl.pallas_call(
        kernel,
        out_shape=(
            V((KP, D), f32),
            V((N,), f32),
        ),
        in_specs=[pl.BlockSpec(memory_space=pl.ANY)] * 2,
        out_specs=[pl.BlockSpec(memory_space=pltpu.VMEM)] * 2,
        scratch_shapes=[
            V((N, D), f32), V((KP, D), f32),
            V((N, D), bf16), V((N, D), bf16), V((D, N), bf16), V((D, N), bf16),
            V((KP, N), f32), V((NT, 8, N), f32), V((NT, 8, N), f32), V((NT, 8, N), f32),
            V((NC, 1, N), f32), V((KP, D), f32), V((KP, 128), f32),
            V((NX, NZ, 128), f32), V((NX - 1, NZ, 128), f32),
            V((NZ, 1, 128), f32), V((NZ - 1, 1, 128), f32),
            V((Q, 8, PA, D), f32), V((Q, 8, 2, PA, D), f32),
            V((Q, PA, D), f32), V((Q, 3, 2, PA, D), f32),
            V((Q, 2, CQ // 2, D), f32), V((3, Q, 2, CQ, D), f32),
            V((Q, NX - 1, PB, D), f32),
            V((RA + RB, RA + RB), f32),
            pltpu.SemaphoreType.DMA((NSEND,)), pltpu.SemaphoreType.DMA((NRECV,)),
            pltpu.SemaphoreType.DMA((NT + 4,)),
        ],
        compiler_params=pltpu.CompilerParams(
            collective_id=0, has_side_effects=True, vmem_limit_bytes=50 * 1024 * 1024
        ),
    )(vectors, centroids)
    return refined, lse * LN2


def solution(mesh):
    return jax.shard_map(
        local,
        mesh=mesh,
        in_specs=(P("item", None), P("cent", None)),
        out_specs=(P("cent", None), P("item")),
        check_vma=False,
    )
```

```python
import functools
import math

import jax
import jax.numpy as jnp
from jax import lax
from jax.experimental import pallas as pl
from jax.experimental.pallas import tpu as pltpu
from jax.sharding import PartitionSpec as P

MESH = pl.DeviceIdType.MESH
BOLTZMANN_SCALE = 8.0
PRIOR = 2.0
LOG2E = math.log2(math.e)
LN2 = math.log(2.0)
XSCALE = 2.0 * LOG2E / BOLTZMANN_SCALE

NX, NZ, NC = 4, 8, 8
D = 256
N = 1024
KP = 4096
RA, RB = 80, 48
CA, CB = NZ * RA, NX * RB
B0 = NX * CA
TB = 768
NTB = NZ * CB // TB
NT = NX + NTB
Q = 2
PA, PB = RA // Q, RB // Q
CQ = NX * PB
HALF_A = (((0, 24), (24, 16)), ((0, 16), (16, 24)))
HALF_B = (((0, 16), (16, 8)), ((0, 8), (8, 16)))

STAT, W1, W2 = range(3)
BX = 3
GBX = BX + Q
A1 = GBX + Q
A2 = A1 + 8 * Q
AZ = A2 + 8 * Q
BZ = AZ + 4 * Q
GAZ = BZ + 4 * Q
GA1 = GAZ + 4 * Q
GA2 = GA1 + 8 * Q
GBZ = GA2 + Q
GBL = GBZ + 12 * Q
NRECV = GBL + Q
S_STAT, S_W1, S_W2, S_BX, S_GBX, S_A1, S_A2, S_AZ, S_BZ, S_GAZ, S_GA1, S_GA2, S_GBZ = range(13)
NSEND = 13

ORDER_RS = (4, 3, -3, 2, -2, 1, -1, 0)
ORDER_AG = (0, -1, 1, -2, 2, -3, 3, 4)
ORDER_T = (0, -1, 1, 2)


def dot(a, b):
    return jnp.dot(a, b, preferred_element_type=jnp.float32)


def dot_t(a, b):
    return lax.dot_general(a, b, (((1,), (1,)), ((), ())), preferred_element_type=jnp.float32)


def split(v):
    hi = v.astype(jnp.bfloat16)
    lo = (v - hi.astype(jnp.float32)).astype(jnp.bfloat16)
    return hi, lo


def kernel(
    x_hbm, c_hbm, out, lse_out,
    xbuf, cbuf, xh, xl, e_buf, m_buf, s_buf, f_buf, stat, numer, w8,
    wown, rw1, w2s, rw2, ra1, ra2, raz0, raz, rbz0, rbz, rbx, den,
    ss, rs, lsem,
):
    item = lax.axis_index("item")
    cent = lax.axis_index("cent")
    x, z = item // NZ, lax.rem(item, NZ)

    def mod(v, n):
        return lax.rem(v + 2 * n, n)

    def at_x(d):
        return {"item": mod(x + d, NX) * NZ + z}

    def at_z(d):
        return {"item": x * NZ + mod(z + d, NZ)}

    def at_c(d):
        return {"cent": mod(cent + d, NC)}

    def copy(src, dst, kind, k, dev):
        return pltpu.make_async_remote_copy(
            src_ref=src, dst_ref=dst, send_sem=ss.at[kind], recv_sem=rs.at[k],
            device_id=dev, device_id_type=MESH,
        )

    def send(src, dst, kind, k, dev):
        copy(src, dst, kind, k, dev).start()

    def got(region, k):
        copy(region, region, 0, k, at_x(1)).wait_recv()

    def sent(region, kind):
        copy(region, region, kind, 0, at_x(1)).wait_send()

    def x_load(j):
        rows = pl.ds(j * 256, 256)
        return pltpu.make_async_copy(x_hbm.at[rows], xbuf.at[rows], lsem.at[NT + j])

    for j in range(N // 256):
        x_load(j).start()

    def tile_rows(t, rows_n, base):
        return pl.ds(pl.multiple_of(base + t * rows_n, 8), rows_n)

    def c_load(t, rows_n, base, k):
        rows = tile_rows(t, rows_n, base)
        return pltpu.make_async_copy(c_hbm.at[rows], cbuf.at[rows], lsem.at[k])

    for t in range(NX):
        c_load(t, CA, 0, t).start()
    for t in range(NTB):
        c_load(t, TB, B0, NX + t).start()

    barrier = pltpu.get_barrier_semaphore()
    for d in range(1, NX):
        pl.semaphore_signal(barrier, inc=1, device_id=at_x(d), device_id_type=MESH)
    for d in range(1, NZ):
        pl.semaphore_signal(barrier, inc=1, device_id=at_z(d), device_id_type=MESH)
    for d in range(1, NC):
        pl.semaphore_signal(barrier, inc=1, device_id=at_c(d), device_id_type=MESH)

    for j in range(N // 256):
        x_load(j).wait()
        rows = pl.ds(j * 256, 256)
        v = xbuf[rows, :] * XSCALE
        hi, lo = split(v)
        xh[rows, :] = hi
        xl[rows, :] = lo

    def stage_a(rows_n, base, first):
        def tile(t, _):
            c_load(t, rows_n, base, first + t).wait()
            rows = tile_rows(t, rows_n, base)
            c = cbuf[rows, :]
            csq = jnp.sum(c * c, axis=1, keepdims=True) * (LOG2E / BOLTZMANN_SCALE)
            ch, cl = split(c)
            for j in range(N // 256):
                cols = pl.ds(j * 256, 256)
                b = xh[cols, :]
                l = dot_t(ch, b) + dot_t(cl, b) + dot_t(ch, xl[cols, :]) - csq
                l = l.reshape(rows_n // 8, 8, 256)
                m = jnp.max(l, axis=0)
                e = jnp.exp2(l - m[None])
                e_buf[rows, cols] = e.reshape(rows_n, 256)
                m_buf[first + t, :, cols] = m
                s_buf[first + t, :, cols] = jnp.sum(e, axis=0)
            return 0

        return tile

    lax.fori_loop(0, NX, stage_a(CA, 0, 0), 0)
    lax.fori_loop(0, NTB, stage_a(TB, B0, NX), 0)

    mm = m_buf[...]
    m_loc = jnp.max(jnp.max(mm, axis=0), axis=0, keepdims=True)
    s_loc = jnp.sum(
        jnp.sum(s_buf[...] * jnp.exp2(mm - m_loc[None]), axis=0), axis=0, keepdims=True
    )
    stat[cent] = m_loc + jnp.log(s_loc) * LOG2E
    pl.semaphore_wait(barrier, (NX - 1) + (NZ - 1) + (NC - 1))
    for d in (4, 3, 5, 2, 6, 1, 7):
        send(stat.at[cent], stat.at[cent], S_STAT, STAT, at_c(d))
    got(stat.at[pl.ds(0, NC - 1)], STAT)
    parts = stat[...]
    top = jnp.max(parts, axis=0)
    total = jnp.log(jnp.sum(jnp.exp2(parts - top[None]), axis=0))
    lse2 = top + total * LOG2E
    lse_out[...] = lse2.reshape(N)
    f_buf[...] = jnp.exp2(mm - lse2[None])

    def block_b(pieces, f):
        hs, ls = [], []
        for rows in pieces:
            n = rows.size
            p = (e_buf[rows, :].reshape(n // 8, 8, N) * f[None]).reshape(n, N)
            w = p[:, 0:128]
            for q in range(1, N // 128):
                w = w + p[:, q * 128 : (q + 1) * 128]
            w8[rows, :] = w
            hi, lo = split(p)
            hs.append(hi)
            ls.append(lo)
        hi = jnp.concatenate(hs, axis=0)
        lo = jnp.concatenate(ls, axis=0)
        r = dot(hi, xh[...]) + dot(lo, xh[...]) + dot(hi, xl[...])
        at = 0
        for rows in pieces:
            numer[rows, :] = r[at : at + rows.size]
            at += rows.size

    def rows_a(dx, dz, l, off=0, n=PA):
        start = mod(x + dx, NX) * CA + l * NZ * PA + mod(z + dz, NZ) * PA + off
        return pl.ds(pl.multiple_of(start, 8), n)

    def rows_b(dz, dx, l, off=0, n=PB):
        start = B0 + mod(z + dz, NZ) * CB + l * CQ + mod(x + dx, NX) * PB + off
        return pl.ds(pl.multiple_of(start, 8), n)

    def chunk_rows_b(dz, off=0, n=CB):
        return pl.ds(pl.multiple_of(B0 + mod(z + dz, NZ) * CB + off, 8), n)

    def add(rows, ref):
        numer[rows, :] += ref[...]

    HQ = CQ // 2
    SIDES = ((0, 1), (1, -1))

    def a1_send(l, i):
        for e, sg in SIDES:
            off, n = HALF_A[l][e]
            send(
                numer.at[rows_a(2, ORDER_RS[i], l, off, n)], ra1.at[l, i, pl.ds(off, n)],
                S_A1, A1 + 8 * l + i, at_x(sg))

    def a1_step(l, i):
        o = ORDER_RS[i]
        got(ra1.at[l, i], A1 + 8 * l + i)
        for e, sg in SIDES:
            off, n = HALF_A[l][e]
            add(rows_a(sg, o, l, off, n), ra1.at[l, i, pl.ds(off, n)])
            send(numer.at[rows_a(sg, o, l)], ra2.at[l, i, e], S_A2, A2 + 8 * l + i, at_x(sg))

    def a2_step(l, i):
        got(ra2.at[l, i], A2 + 8 * l + i)
        numer[rows_a(0, ORDER_RS[i], l), :] += ra2[l, i, 0] + ra2[l, i, 1]

    def az_send0(l):
        for e, sg in SIDES:
            off, n = HALF_A[l][e]
            send(
                numer.at[rows_a(0, 4, l, off, n)], raz0.at[l, pl.ds(off, n)],
                S_AZ, AZ + 4 * l, at_z(sg))

    def az_step(l, k):
        got(raz0.at[l] if k == 1 else raz.at[l, k - 2], AZ + 4 * l + k - 1)
        for e, sg in SIDES:
            if k == 1:
                off, n = HALF_A[l][e]
                add(rows_a(0, 3 * sg, l, off, n), raz0.at[l, pl.ds(off, n)])
            else:
                add(rows_a(0, (4 - k) * sg, l), raz.at[l, k - 2, e])
            send(
                numer.at[rows_a(0, (4 - k) * sg, l)], raz.at[l, k - 1, e],
                S_AZ, AZ + 4 * l + k, at_z(sg))

    def bz_send0(q):
        for e, sg in SIDES:
            send(
                numer.at[chunk_rows_b(4, q * CQ + e * HQ, HQ)], rbz0.at[q, e],
                S_BZ, BZ + 4 * q, at_z(sg))

    def bz_step(k, q):
        got(rbz0.at[q] if k == 1 else rbz.at[k - 2, q], BZ + 4 * q + k - 1)
        for e, sg in SIDES:
            if k == 1:
                add(chunk_rows_b(3 * sg, q * CQ + e * HQ, HQ), rbz0.at[q, e])
            else:
                add(chunk_rows_b((4 - k) * sg, q * CQ, CQ), rbz.at[k - 2, q, e])
            send(
                numer.at[chunk_rows_b((4 - k) * sg, q * CQ, CQ)], rbz.at[k - 1, q, e],
                S_BZ, BZ + 4 * q + k, at_z(sg))

    def bz_last(q):
        got(rbz.at[2, q], BZ + 4 * q + 3)
        numer[chunk_rows_b(0, q * CQ, CQ), :] += rbz[2, q, 0] + rbz[2, q, 1]

    def owner_weights(xd, zd):
        a, b = xd * CA + zd * PA, B0 + zd * CB + xd * PB
        rows = [pl.ds(a + l * NZ * PA, PA) for l in range(Q)] + [pl.ds(b + l * CQ, PB) for l in range(Q)]
        t = jnp.concatenate([w8[r, :] for r in rows], axis=0).T
        wown[xd, zd : zd + 1, :] = jnp.sum(t, axis=0, keepdims=True)

    def weights(k):
        for i in range(8 * k, 8 * k + 8):
            owner_weights(*divmod(i, NZ))

    def weights_x():
        for d in range(1, NX):
            send(wown.at[mod(x + d, NX)], rw1.at[d - 1], S_W1, W1, at_x(d))

    def weights_z():
        got(rw1, W1)
        w = wown[x] + rw1[0] + rw1[1] + rw1[2]
        for s in range(NZ):
            w2s[s] = w[s : s + 1, :]
        for d in range(1, NZ):
            send(w2s.at[mod(z + d, NZ)], rw2.at[d - 1], S_W2, W2, at_z(d))

    def weights_own():
        got(rw2, W2)
        w = w2s[z]
        for d in range(1, NZ):
            w = w + rw2[d - 1]
        den[...] = jnp.broadcast_to(w, (RA + RB, RA + RB)).T + PRIOR

    def bx_send(l):
        for d in range(1, NX):
            send(numer.at[rows_b(0, d, l)], rbx.at[l, d - 1], S_BX, BX + l, at_x(d))

    def finish(mine, rows, total_rows):
        q = den[mine, :]
        q = jnp.concatenate([q, q], axis=1)
        out[rows, :] = (total_rows * (1.0 / XSCALE) + PRIOR * cbuf[rows, :]) / q

    def finish_b(l):
        got(rbx.at[l], BX + l)
        rows = rows_b(0, 0, l)
        finish(pl.ds(RA + l * PB, PB), rows, numer[rows, :] + rbx[l, 0] + rbx[l, 1] + rbx[l, 2])

    def finish_a(l):
        got(raz.at[l, 2], AZ + 4 * l + 3)
        rows = rows_a(0, 0, l)
        finish(pl.ds(l * PA, PA), rows, numer[rows, :] + raz[l, 2, 0] + raz[l, 2, 1])

    def give(rows, kind, k, dev):
        send(out.at[rows], out.at[rows], kind, k, dev)

    def gaz_send(l, k):
        for e, sg in SIDES:
            rows = rows_a(0, -k * sg, l) if k < 3 else rows_a(0, -3 * sg, l, *HALF_A[l][e])
            give(rows, S_GAZ, GAZ + 4 * l + k, at_z(sg))

    def gaz_got(l, k):
        got(numer.at[pl.ds(0, 2 * PA if k < 3 else PA)], GAZ + 4 * l + k)

    def ga1_send(l, i):
        for _, sg in SIDES:
            give(rows_a(0, ORDER_AG[i], l), S_GA1, GA1 + 8 * l + i, at_x(sg))

    def ga1_got(l, i):
        got(numer.at[pl.ds(0, 2 * PA)], GA1 + 8 * l + i)

    def ga2_send(l, i):
        give(rows_a(0, ORDER_AG[i], l), S_GA2, GA2 + l, at_x(2))

    def ga2_step(l, i):
        ga1_got(l, i)
        for e, sg in SIDES:
            give(rows_a(-sg, ORDER_AG[i], l, *HALF_A[l][e]), S_GA2, GA2 + l, at_x(sg))

    def gbx_send(l):
        for d in (2, 1, 3):
            give(rows_b(0, 0, l), S_GBX, GBX + l, at_x(d))

    def gbz_send(l, k, j):
        t = ORDER_T[j]
        for e, sg in SIDES:
            if k < 3:
                give(rows_b(-k * sg, t, l), S_GBZ, GBZ + 12 * l + 3 * j + k, at_z(sg))
            else:
                give(rows_b(-3 * sg, t, l, *HALF_B[l][e]), S_GBZ, GBL + l, at_z(sg))

    def gbz_first(l):
        got(numer.at[pl.ds(0, 3 * PB)], GBX + l)
        for j in (1, 2, 3):
            gbz_send(l, 0, j)

    def gbz_step(l, k, j):
        got(numer.at[pl.ds(0, 2 * PB)], GBZ + 12 * l + 3 * j + k)
        gbz_send(l, k + 1, j)

    def part_a(dx, l):
        start = mod(x + dx, NX) * CA + l * NZ * PA
        block_b([pl.ds(pl.multiple_of(start, 8), NZ * PA)], f_buf[mod(x + dx, NX)])

    def part_b(dz):
        block_b([chunk_rows_b(dz)], f_buf[NX + mod(z + dz, NZ) // (NZ // NTB)])

    part_b(4)
    bz_send0(0)
    bz_send0(1)
    part_a(2, 0)
    a1_send(0, 0)
    a1_send(0, 1)
    part_a(2, 1)
    a1_send(1, 3)
    a1_send(1, 0)
    a1_send(1, 1)
    part_b(3)
    part_b(-3)
    part_a(1, 0)
    part_a(-1, 0)
    a1_send(0, 2)
    a1_send(1, 2)
    bz_step(1, 0)
    a1_step(0, 0)
    a1_send(0, 4)
    a1_send(1, 4)
    part_a(1, 1)
    bz_step(1, 1)
    a1_send(0, 3)
    part_a(-1, 1)
    a1_step(1, 0)
    a1_step(1, 1)
    part_a(0, 1)
    a1_step(0, 1)
    a1_step(0, 2)
    part_b(-2)
    a1_step(1, 2)
    part_a(0, 0)
    a1_send(0, 5)
    a2_step(0, 0)
    az_send0(0)
    a1_send(0, 6)
    part_b(2)
    bz_step(2, 0)
    a1_step(0, 4)
    a1_step(1, 4)
    a1_send(1, 5)
    a1_send(1, 6)
    a1_step(0, 3)
    a1_send(1, 7)
    a1_send(0, 7)
    a1_step(1, 3)
    part_b(-1)
    a2_step(1, 0)
    az_send0(1)
    part_b(1)
    bz_step(2, 1)
    part_b(0)
    a2_step(1, 1)
    weights(0)
    weights(1)
    weights(2)
    weights(3)
    a2_step(0, 1)
    weights_x()
    a2_step(0, 2)
    az_step(0, 1)
    bz_step(3, 0)
    a2_step(1, 2)
    az_step(1, 1)
    a1_step(0, 5)
    a1_step(0, 6)
    a2_step(0, 4)
    bz_step(3, 1)
    a2_step(1, 4)
    a1_step(1, 5)
    a1_step(1, 6)
    a2_step(0, 3)
    az_step(0, 2)
    a1_step(1, 7)
    a1_step(0, 7)
    bz_last(0)
    bx_send(0)
    a2_step(1, 3)
    az_step(1, 2)
    weights_z()
    a2_step(0, 5)
    a2_step(0, 6)
    bz_last(1)
    bx_send(1)
    a2_step(1, 5)
    az_step(0, 3)
    a2_step(1, 6)
    az_step(1, 3)
    weights_own()
    a2_step(1, 7)
    a2_step(0, 7)
    finish_b(0)
    gbz_send(0, 0, 0)
    finish_a(0)
    gaz_send(0, 0)
    gbx_send(0)
    ga1_send(0, 0)
    finish_b(1)
    gbx_send(1)
    finish_a(1)
    ga1_send(1, 0)
    gaz_send(1, 0)
    gbz_send(1, 0, 0)
    gbz_step(0, 0, 0)
    gaz_got(0, 0)
    gaz_send(0, 1)
    ga1_send(0, 1)
    gbz_first(0)
    ga1_send(0, 2)
    gaz_got(1, 0)
    gaz_send(1, 1)
    ga1_send(1, 2)
    ga1_send(1, 1)
    ga2_step(0, 0)
    gbz_step(1, 0, 0)
    gbz_first(1)
    gbz_step(0, 1, 0)
    ga2_step(1, 0)
    gaz_got(0, 1)
    gaz_send(0, 2)
    ga1_send(0, 3)
    ga2_step(0, 1)
    ga1_send(0, 4)
    gbz_step(0, 0, 3)
    ga2_step(0, 2)
    gbz_step(0, 0, 2)
    gbz_step(0, 0, 1)
    ga2_step(1, 2)
    gaz_got(1, 1)
    gaz_send(1, 2)
    ga1_send(1, 4)
    ga2_step(1, 1)
    ga1_send(1, 3)
    gbz_step(1, 1, 0)
    gbz_step(1, 0, 3)
    gbz_step(1, 0, 2)
    ga2_step(0, 3)
    gbz_step(1, 0, 1)
    gbz_step(0, 2, 0)
    ga2_step(0, 4)
    gaz_got(0, 2)
    gaz_send(0, 3)
    ga1_send(0, 6)
    ga1_send(0, 5)
    gbz_step(0, 1, 3)
    gbz_step(0, 1, 2)
    gbz_step(0, 1, 1)
    ga2_step(1, 4)
    gaz_got(1, 2)
    gaz_send(1, 3)
    ga1_send(1, 6)
    ga1_send(1, 5)
    ga2_step(1, 3)
    gbz_step(1, 2, 0)
    gbz_step(1, 1, 3)
    gbz_step(1, 1, 2)
    gbz_step(1, 1, 1)
    ga2_step(0, 6)
    gaz_got(0, 3)
    ga1_send(0, 7)
    ga2_step(0, 5)
    gbz_step(0, 2, 3)
    gbz_step(0, 2, 2)
    gbz_step(0, 2, 1)
    ga2_step(1, 6)
    gaz_got(1, 3)
    ga1_send(1, 7)
    ga2_send(1, 7)
    ga2_step(1, 5)
    gbz_step(1, 2, 3)
    gbz_step(1, 2, 2)
    gbz_step(1, 2, 1)
    ga2_step(0, 7)
    for l in range(Q):
        got(numer.at[pl.ds(0, NX * PB)], GBL + l)
        got(numer.at[pl.ds(0, 8 * PA)], GA2 + l)
    ga1_got(1, 7)

    sent(stat.at[pl.ds(0, NC - 1)], S_STAT)
    sent(rw1, S_W1)
    sent(rw2, S_W2)
    sent(rbx, S_BX)
    sent(rbx, S_GBX)
    sent(ra1, S_A1)
    sent(ra2, S_A2)
    for kind, rows in (
        (S_AZ, 7 * RA), (S_GAZ, 7 * RA), (S_GA1, 16 * RA), (S_GA2, 8 * RA),
        (S_BZ, 7 * CB), (S_GBZ, 7 * CB),
    ):
        sent(numer.at[pl.ds(0, rows)], kind)


def local(vectors, centroids):
    f32, bf16 = jnp.float32, jnp.bfloat16
    V = pltpu.VMEM
    refined, lse = pl.pallas_call(
        kernel,
        out_shape=(
            V((KP, D), f32),
            V((N,), f32),
        ),
        in_specs=[pl.BlockSpec(memory_space=pl.ANY)] * 2,
        out_specs=[pl.BlockSpec(memory_space=pltpu.VMEM)] * 2,
        scratch_shapes=[
            V((N, D), f32), V((KP, D), f32),
            V((N, D), bf16), V((N, D), bf16),
            V((KP, N), f32), V((NT, 8, N), f32), V((NT, 8, N), f32), V((NT, 8, N), f32),
            V((NC, 1, N), f32), V((KP, D), f32), V((KP, 128), f32),
            V((NX, NZ, 128), f32), V((NX - 1, NZ, 128), f32),
            V((NZ, 1, 128), f32), V((NZ - 1, 1, 128), f32),
            V((Q, 8, PA, D), f32), V((Q, 8, 2, PA, D), f32),
            V((Q, PA, D), f32), V((Q, 3, 2, PA, D), f32),
            V((Q, 2, CQ // 2, D), f32), V((3, Q, 2, CQ, D), f32),
            V((Q, NX - 1, PB, D), f32),
            V((RA + RB, RA + RB), f32),
            pltpu.SemaphoreType.DMA((NSEND,)), pltpu.SemaphoreType.DMA((NRECV,)),
            pltpu.SemaphoreType.DMA((NT + 4,)),
        ],
        compiler_params=pltpu.CompilerParams(
            collective_id=0, has_side_effects=True, vmem_limit_bytes=50 * 1024 * 1024
        ),
    )(vectors, centroids)
    return refined, lse * LN2


def solution(mesh):
    return jax.shard_map(
        local,
        mesh=mesh,
        in_specs=(P("item", None), P("cent", None)),
        out_specs=(P("cent", None), P("item")),
        check_vma=False,
    )
```
